256 devices in a mesh: dp: 4 (over x), fsdp: 16 (over z_hi, y, core), mp: 4 (over z_lo).
Axes of the slice: x: 4, y: 4, z: 8 (z_hi: 2, z_lo: 4; z = z_hi * 4 + z_lo), core: 2. Of those that a mesh axis runs over, the one named last changes fastest.
Arguments:
- tokens_in: bfloat16 [512, 8192], P('dp', 'fsdp'), may hold values from -5 to 5
- weight: bfloat16 [8192, 4, 8192], P('fsdp', 'dp', 'mp'), may hold values from -0.25 to 0.25
- cotangent: bfloat16 [512, 4, 8192], P('dp', None, 'mp'), may hold values from -5 to 5
- row_moment: float32 [8192], P('fsdp'), may hold values from 0.01 to 1
- col_moment: float32 [4, 8192], P('dp', 'mp'), may hold values from 0.01 to 1
Outputs:
- input_grad: bfloat16 [512, 8192], P('dp', ('fsdp', 'mp'))
- row_moment_new: float32 [8192], P('fsdp')
- col_moment_new: float32 [4, 8192], P('dp', 'mp')
- update: float32 [8192, 4, 8192], P('fsdp', 'dp', 'mp')
- update_rms: float32 [], replicated
The draws below stay inside these ranges and needn't reach their ends.
All inputs are finite; a program needn't handle non-finite values.
Results may differ from the reference program's by a relative error of at most 0.0049.
Values may be sent and summed in bfloat16 or wider, within the bound.
A program may use at most 64 MiB of HBM per device.

```python
import math
import jax
import jax.numpy as jnp
from jax import lax

D = 8192
HID = 32768
STEP_INDEX = 10
TOKENS = 512
FC = 8192
N_DP = 4


def scaled_field(key, rows, width):
    key_a, key_b = jax.random.split(key, 2)
    positions = jnp.arange(width, dtype=jnp.float32) / width
    spread = 0.5 * positions + 0.5 * jax.random.uniform(key_a, (width,))
    col_scale = 0.08 * 10.0 ** spread
    values = jnp.clip(jax.random.normal(key_b, (rows, width)), -6.0, 6.0)
    return jnp.clip(values * col_scale, -4.9, 4.9)


def draw_tokens_in(key, part):
    key = jax.random.fold_in(key, 11)
    return scaled_field(key, TOKENS, D).astype(jnp.bfloat16)


def draw_cotangent(key, part):
    key = jax.random.fold_in(key, 23)
    return scaled_field(key, TOKENS, HID).reshape(TOKENS, N_DP, FC).astype(jnp.bfloat16)


def block_scale(own_key, dims, pieces, least, top_value):
    def one(position, blocks):
        heights = jax.random.uniform(jax.random.fold_in(jax.random.fold_in(own_key, 6), position), (blocks,), jnp.float32, least / len(pieces), top_value / len(pieces))
        return jnp.repeat(jnp.exp(heights), dims[position] // blocks).reshape((-1,) + (1,) * (len(dims) - position - 1))

    level = one(*pieces[0])
    for cut in pieces[1:]:
        level = level * one(*cut)
    return level


def scatter_about(stream_key, shape, scale, reach, cuts=(), kind=jnp.bfloat16):
    array = scale * jax.random.normal(stream_key, shape, jnp.float32)
    if cuts:
        array = array * block_scale(stream_key, shape, cuts, -0.22, 0.18)
    return jnp.clip(array, -reach, reach).astype(kind)


def setup_inputs(seed: int = 0) -> dict:
    keys = jax.random.split(jax.random.key(seed), 6)
    tokens_in = draw_tokens_in(jax.random.fold_in(keys[5], 71), 0)
    weight = scatter_about(keys[1], (D, N_DP, FC), (D // 16) ** -0.5, 0.25, ((0, 16), (1, 4), (2, 4)))
    cotangent = draw_cotangent(jax.random.fold_in(keys[5], 71), 0)
    row_moment = jnp.clip(jnp.exp(math.log(1.0) - 4.6051702 * jax.random.uniform(keys[3], (D,), jnp.float32) ** block_scale(keys[3], (D,), ((0, 16),), -0.2, 0.2)), 0.01, 1.0)
    col_moment = jnp.clip(jnp.exp(math.log(1.0) - 4.6051702 * jax.random.uniform(keys[4], (N_DP, FC), jnp.float32) ** block_scale(keys[4], (N_DP, FC), ((0, 4), (1, 4)), -0.2, 0.2)), 0.01, 1.0)
    return dict(tokens_in=tokens_in, weight=weight, cotangent=cotangent, row_moment=row_moment, col_moment=col_moment)


tiny_term = 1e-30
clip_level = 1.0
gelu_coeff = 0.044715

def gelu_slope(values):
    root_term = math.sqrt(2.0 / math.pi)
    tanh_value = jnp.tanh(root_term * (values + gelu_coeff * values * values * values))
    return 0.5 * (1.0 + tanh_value) + 0.5 * values * (1.0 - tanh_value * tanh_value) * root_term * (1.0 + 3.0 * gelu_coeff * values * values)

def reference(tokens_in, weight, cotangent, row_moment, col_moment):
    weight_flat = weight.reshape(D, HID)
    grad_out = cotangent.reshape(TOKENS, HID)
    hidden = jnp.dot(tokens_in, weight_flat, preferred_element_type=jnp.float32)
    slope = (grad_out.astype(jnp.float32) * gelu_slope(hidden)).astype(jnp.bfloat16)
    input_grad = jnp.dot(slope, weight_flat.T, preferred_element_type=jnp.float32).astype(jnp.bfloat16)
    gradient = jnp.dot(tokens_in.T, slope, preferred_element_type=jnp.float32)
    squares = gradient * gradient + tiny_term
    decay_rate = 1.0 - STEP_INDEX ** (-0.8)
    row_new = decay_rate * row_moment + (1.0 - decay_rate) * lax.optimization_barrier(jnp.mean(squares, axis=1))
    col_new = decay_rate * col_moment.reshape(HID) + (1.0 - decay_rate) * lax.optimization_barrier(jnp.mean(squares, axis=0))
    second = row_new[:, None] * col_new[None, :] / jnp.mean(row_new)
    normalized = gradient / jnp.sqrt(second)
    update_rms = jnp.sqrt(jnp.mean(normalized * normalized))
    update = normalized / jnp.maximum(1.0, update_rms / clip_level)
    return (input_grad, row_new, col_new.reshape(N_DP, FC), update.reshape(D, N_DP, FC), update_rms)
```

```python
import math

import jax
import jax.numpy as jnp
from jax import lax
from jax.sharding import PartitionSpec as P

D = 8192
HID = 32768
STEP_INDEX = 10


tiny_term = 1e-30
clip_level = 1.0
gelu_coeff = 0.044715


def gelu_slope(values):
    root_term = math.sqrt(2.0 / math.pi)
    tanh_value = jnp.tanh(root_term * (values + gelu_coeff * values * values * values))
    return 0.5 * (1.0 + tanh_value) + 0.5 * values * (1.0 - tanh_value * tanh_value) * root_term * (
        1.0 + 3.0 * gelu_coeff * values * values
    )


def per_device(tokens_in, weight, cotangent, row_moment, col_moment):
    tok_here = tokens_in.shape[0]
    fsdp_count = lax.axis_size("fsdp")
    dp_count = lax.axis_size("dp")
    decay_rate = 1.0 - STEP_INDEX ** (-0.8)
    share = tok_here // fsdp_count
    own = weight[:, 0, :]
    tokens = lax.all_gather(tokens_in, "dp", axis=0, tiled=True)
    hidden = jnp.dot(tokens, own, preferred_element_type=jnp.float32)
    hidden = hidden.reshape(dp_count, fsdp_count, share, -1).swapaxes(0, 1).reshape(hidden.shape)
    hidden = lax.psum_scatter(hidden, "fsdp", scatter_dimension=0, tiled=True)
    offset = lax.axis_index("fsdp") * share
    upstream = lax.dynamic_slice_in_dim(cotangent, offset, share, 0).swapaxes(0, 1)
    upstream = lax.all_to_all(upstream, "dp", split_axis=0, concat_axis=0, tiled=True)
    upstream = upstream.reshape(hidden.shape)
    slope = (upstream.astype(jnp.float32) * gelu_slope(hidden)).astype(jnp.bfloat16)
    slope = lax.all_gather(slope, "fsdp", axis=0, tiled=True)
    slope = slope.reshape(fsdp_count, dp_count, share, -1).swapaxes(0, 1).reshape(slope.shape)
    input_terms = jnp.dot(slope, own.T, preferred_element_type=jnp.float32)
    gradient = jnp.dot(tokens.T, slope, preferred_element_type=jnp.float32)
    input_grad = lax.psum_scatter(input_terms, "dp", scatter_dimension=0, tiled=True)
    input_grad = lax.psum_scatter(input_grad, "mp", scatter_dimension=1, tiled=True)
    input_grad = input_grad.astype(jnp.bfloat16)
    squares = gradient * gradient + tiny_term
    row_total = lax.psum(jnp.sum(squares, axis=1), ("dp", "mp"))
    col_total = lax.psum(jnp.sum(squares, axis=0), "fsdp")
    row_new = decay_rate * row_moment + (1.0 - decay_rate) * row_total / HID
    col_new = decay_rate * col_moment + (1.0 - decay_rate) * col_total[None] / D
    shape = gradient * lax.rsqrt(row_new)[:, None] * lax.rsqrt(col_new)
    totals = jnp.stack([jnp.sum(row_new) / 16.0, jnp.sum(shape * shape)])
    totals = lax.psum(totals, ("dp", "fsdp", "mp"))
    row_mean = totals[0] / D
    update_rms = jnp.sqrt(row_mean * totals[1] / (D * HID))
    factor = jnp.sqrt(row_mean) / jnp.maximum(1.0, update_rms / clip_level)
    update = (shape * factor)[:, None, :]
    return (input_grad, row_new, col_new, update, update_rms)


def solution(mesh):
    in_specs = (
        P("dp", "fsdp"),
        P("fsdp", "dp", "mp"),
        P("dp", None, "mp"),
        P("fsdp"),
        P("dp", "mp"),
    )
    out_specs = (P("dp", ("fsdp", "mp")), P("fsdp"), P("dp", "mp"), P("fsdp", "dp", "mp"), P())
    return jax.shard_map(
        per_device, mesh=mesh, in_specs=in_specs, out_specs=out_specs, check_vma=False
    )
```

```python
import math

import jax
import jax.numpy as jnp
from jax import lax
from jax.experimental import pallas as pl
from jax.experimental.pallas import tpu as pltpu
from jax.sharding import PartitionSpec as P

MESH = pl.DeviceIdType.MESH
D = 8192
HID = 32768
STEP_INDEX = 10
DECAY = 1.0 - STEP_INDEX ** (-0.8)

tiny_term = 1e-30
clip_level = 1.0
gelu_coeff = 0.044715

F32 = jnp.float32
BF16 = jnp.bfloat16

CHUNK = 128
HALF = 64
COLS = 256
ROWS = 512
GROUPS = 8
ORDER = (0, 1, 3, 2)
UP = (0, 1)


def gelu_slope(values):
    root_term = math.sqrt(2.0 / math.pi)
    tanh_value = jnp.tanh(root_term * (values + gelu_coeff * values * values * values))
    return 0.5 * (1.0 + tanh_value) + 0.5 * values * (1.0 - tanh_value * tanh_value) * root_term * (
        1.0 + 3.0 * gelu_coeff * values * values
    )


class Slots:
    def __init__(self):
        self.numbers = {}

    def __call__(self, *key):
        return self.numbers.setdefault(key, len(self.numbers))


N_SEMS = 112


def main_kernel(
    tok, wgt, cot, row_mom, col_mom,
    grad_out, inp_out, row_out, rcol_out, col_out, scal_out,
    t_own, t_peer, t_tr, w_own, w_peer, ct,
    sd, rd, sn, rm, rp, hn, ho, zs, zr, sl, grad, terms,
    i_out, i_in, i_sum, j_out, j_in,
    row_acc, row_buf, col_buf, one_buf, two_buf,
    send, recv, local, peer_send, peer_recv,
):
    d, f, m = lax.axis_index("dp"), lax.axis_index("fsdp"), lax.axis_index("mp")
    c, y, zh = f % 2, (f // 2) % 4, f // 8
    fid = lambda zz, yy, cc: (zz * 4 + yy) * 2 + cc
    core_dev = {"fsdp": fid(zh, y, 1 - c)}
    up_dev = {"fsdp": fid(zh, (y + 1) % 4, c)}
    down_dev = {"fsdp": fid(zh, (y + 3) % 4, c)}
    z_dev = {"fsdp": fid(1 - zh, y, c)}
    number = Slots()
    sent = []

    def start(src, dst, key, dev):
        i = number(*key)
        copy = pltpu.make_async_remote_copy(
            src_ref=src, dst_ref=dst, send_sem=send.at[i], recv_sem=recv.at[i],
            device_id=dev, device_id_type=MESH,
        )
        copy.start()
        sent.append(copy)

    def wait(dst, key):
        i = number(*key)
        pltpu.make_async_remote_copy(
            src_ref=dst, dst_ref=dst, send_sem=send.at[i], recv_sem=recv.at[i],
            device_id=core_dev, device_id_type=MESH,
        ).wait_recv()

    def x_dev(r):
        return {"dp": (d + r) % 4}

    w_loads = {}
    for rel in (2, 3, 1, 0):
        for cc in (0, 1):
            g = (c if cc == 0 else 1 - c) * 4 + (y + rel) % 4
            copy = pltpu.make_async_copy(
                wgt.at[:, pl.ds(pl.multiple_of(g * COLS, COLS), COLS)], w_own.at[g],
                local.at[rel * 2 + cc],
            )
            copy.start()
            w_loads[rel, cc] = copy
    t_load = pltpu.make_async_copy(tok, t_own.at[d], local.at[8])
    t_load.start()
    c_load = pltpu.make_async_copy(cot.at[d], ct.at[d], local.at[9])
    c_load.start()

    barrier = pltpu.get_barrier_semaphore()

    def greet(j, carry):
        pl.semaphore_signal(barrier, inc=1, device_id={"fsdp": (f + j) % 16}, device_id_type=MESH)
        pl.semaphore_signal(
            barrier, inc=1, device_id={"dp": (d + j // 4) % 4, "mp": (m + j % 4) % 4},
            device_id_type=MESH,
        )
        return carry

    lax.fori_loop(1, 16, greet, 0)
    pl.semaphore_wait(barrier, 30)

    for r in (1, 3, 2):
        start(tok, t_own.at[d], ("tok", r), x_dev(r))
    start(tok, t_peer.at[d], ("tpeer", 0), core_dev)
    for rel in (2, 3, 1, 0):
        yy = (y + rel) % 4
        g = (1 - c) * 4 + yy
        start(
            wgt.at[:, pl.ds(pl.multiple_of(g * COLS, COLS), COLS)], w_peer.at[yy],
            ("w", rel), core_dev,
        )
    for r in (1, 3, 2):
        start(cot.at[(d + r) % 4], ct.at[d], ("ct", r), x_dev(r))

    have_w = set()

    def product(k, rel):
        dk, yy = (d + k) % 4, (y + rel) % 4
        if rel not in have_w:
            have_w.add(rel)
            w_loads[rel, 0].wait()
            wait(w_peer.at[yy], ("w", rel))
        return jnp.dot(
            t_own[dk], w_own[c * 4 + yy], preferred_element_type=F32
        ) + jnp.dot(t_peer[dk], w_peer[yy], preferred_element_type=F32)

    def stage_tokens(k):
        dk = (d + k) % 4
        if k == 0:
            t_load.wait()
        else:
            wait(t_own.at[dk], ("tok", 4 - k))
            start(t_own.at[dk], t_peer.at[dk], ("tpeer", k), core_dev)

    def stage_products(k):
        dk = (d + k) % 4
        wait(t_peer.at[dk], ("tpeer", k))
        sd[k] = product(k, 2).astype(BF16)
        start(sd.at[k], rd.at[k], ("rd", k), up_dev if k in UP else down_dev)
        if k in UP:
            sn[k, 0] = product(k, 3).astype(BF16)
            start(sn.at[k, 0], rp.at[k], ("rp", k), down_dev)
            hn[k] = product(k, 1)
        else:
            sn[k, 0] = product(k, 1).astype(BF16)
            start(sn.at[k, 0], rm.at[k], ("rm", k), up_dev)
            hn[k] = product(k, 3)
        ho[k] = product(k, 0)

    def stage_diagonal(k):
        wait(rd.at[k], ("rd", k))
        sn[k, 1] = (hn[k] + rd[k].astype(F32)).astype(BF16)
        if k in UP:
            start(sn.at[k, 1], rm.at[k], ("rm", k), up_dev)
        else:
            start(sn.at[k, 1], rp.at[k], ("rp", k), down_dev)

    mine = pl.ds(pl.multiple_of(zh * HALF, HALF), HALF)
    other = pl.ds(pl.multiple_of((1 - zh) * HALF, HALF), HALF)

    def stage_sum(k):
        wait(rm.at[k], ("rm", k))
        wait(rp.at[k], ("rp", k))
        ho[k] = ho[k] + rm[k].astype(F32) + rp[k].astype(F32)
        zs[k] = ho[k, other].astype(BF16)
        start(zs.at[k], zr.at[k], ("z", k), z_dev)

    g_own = c * 4 + y

    def rows_of(k, zz):
        dk = (d + k) % 4
        return pl.ds(pl.multiple_of(dk * CHUNK + zz * HALF, HALF), HALF)

    def chunk_of(k):
        dk = (d + k) % 4
        return pl.ds(pl.multiple_of(dk * CHUNK, CHUNK), CHUNK)

    def stage_slope(k):
        dk = (d + k) % 4
        wait(zr.at[k], ("z", k))
        if k == 0:
            c_load.wait()
        else:
            wait(ct.at[dk], ("ct", 4 - k))
        hidden = ho[k, mine] + zr[k].astype(F32)
        sl[g_own, rows_of(k, zh)] = (ct[dk].astype(F32) * gelu_slope(hidden)).astype(BF16)
        block = sl.at[g_own, rows_of(k, zh)]
        start(block, block, ("zs", k), z_dev)

    def stage_spread(k):
        wait(sl.at[g_own, rows_of(k, 1 - zh)], ("zs", k))
        block = sl.at[g_own, chunk_of(k)]
        start(block, block, ("am", k), up_dev)
        start(block, block, ("ap", k), down_dev)
        start(block, block, ("core", 0, k), core_dev)

    def stage_down(k):
        block = sl.at[c * 4 + (y + 3) % 4, chunk_of(k)]
        wait(block, ("am", k))
        if k in UP:
            start(block, block, ("ad", k), up_dev)
        start(block, block, ("core", 3, k), core_dev)

    def stage_up(k):
        block = sl.at[c * 4 + (y + 1) % 4, chunk_of(k)]
        wait(block, ("ap", k))
        if k not in UP:
            start(block, block, ("ad", k), down_dev)
        start(block, block, ("core", 1, k), core_dev)

    def stage_far(k):
        block = sl.at[c * 4 + (y + 2) % 4, chunk_of(k)]
        wait(block, ("ad", k))
        start(block, block, ("core", 2, k), core_dev)

    first = []

    def group(rel, cc):
        g = (c if cc == 0 else 1 - c) * 4 + (y + rel) % 4
        if cc == 1:
            w_loads[rel, 1].wait()
            for k in ORDER:
                wait(sl.at[g, chunk_of(k)], ("core", rel, k))
        value = jnp.dot(t_tr[...], sl[g], preferred_element_type=F32)
        grad[g] = value
        copy = pltpu.make_async_copy(grad.at[g], grad_out.at[g], local.at[10 + rel * 2 + cc])
        copy.start()
        squares = value * value + tiny_term
        col_buf[f, g] = jnp.sum(squares, axis=0, keepdims=True)
        lanes = squares[:, :128] + squares[:, 128:]
        part = lax.dot_general(
            sl[g], w_own[g], (((1,), (1,)), ((), ())), preferred_element_type=F32
        )
        if first:
            row_acc[...] += lanes
            terms[...] += part
        else:
            row_acc[...] = lanes
            terms[...] = part
        first.append(copy)

    stages = (stage_products, stage_diagonal, stage_sum, stage_slope, stage_spread)
    stage_tokens(0)
    for step in range(4 + len(stages) - 1):
        if step == 0:
            stage_products(ORDER[0])
            stage_tokens(1)
            stage_tokens(3)
            continue
        if step == 2:
            stage_tokens(2)
        for s, stage in enumerate(stages):
            if 0 <= step - s < 4:
                stage(ORDER[step - s])
        if step == 3:
            for k in ORDER:
                dk = (d + k) % 4
                t_tr[:, pl.ds(pl.multiple_of(dk * CHUNK, CHUNK), CHUNK)] = t_own[dk].T
    for k in ORDER:
        stage_down(k)
        stage_up(k)
        if k == 1:
            group(0, 0)
    group(0, 1)
    group(3, 0)
    stage_far(0)
    stage_far(1)
    group(1, 0)
    stage_far(3)
    stage_far(2)
    group(3, 1)
    group(1, 1)
    group(2, 0)
    group(2, 1)

    me = d * 4 + m
    row_buf[me] = jnp.sum(row_acc[...].T, axis=0, keepdims=True)

    def to_fsdp(buf, slot, base):
        def one(j, carry):
            pltpu.make_async_remote_copy(
                src_ref=buf.at[slot], dst_ref=buf.at[slot], send_sem=peer_send.at[base + j],
                recv_sem=peer_recv.at[base + j], device_id={"fsdp": (f + j) % 16},
                device_id_type=MESH,
            ).start()
            return carry

        lax.fori_loop(1, 16, one, 0)

    def from_fsdp(buf, base):
        def one(j, carry):
            came = (f + 16 - j) % 16
            pltpu.make_async_remote_copy(
                src_ref=buf.at[came], dst_ref=buf.at[came], send_sem=peer_send.at[base + j],
                recv_sem=peer_recv.at[base + j], device_id={"fsdp": (f + j) % 16},
                device_id_type=MESH,
            ).wait()
            return carry

        lax.fori_loop(1, 16, one, 0)

    def to_plane(buf, slot, base):
        def one(j, carry):
            pltpu.make_async_remote_copy(
                src_ref=buf.at[slot], dst_ref=buf.at[slot], send_sem=peer_send.at[base + j],
                recv_sem=peer_recv.at[base + j],
                device_id={"dp": (d + j // 4) % 4, "mp": (m + j % 4) % 4},
                device_id_type=MESH,
            ).start()
            return carry

        lax.fori_loop(1, 16, one, 0)

    def from_plane(buf, base):
        def one(j, carry):
            came = ((d + 4 - j // 4) % 4) * 4 + (m + 4 - j % 4) % 4
            pltpu.make_async_remote_copy(
                src_ref=buf.at[came], dst_ref=buf.at[came], send_sem=peer_send.at[base + j],
                recv_sem=peer_recv.at[base + j],
                device_id={"dp": (d + j // 4) % 4, "mp": (m + j % 4) % 4},
                device_id_type=MESH,
            ).wait()
            return carry

        lax.fori_loop(1, 16, one, 0)

    to_plane(row_buf, me, 0)
    to_fsdp(col_buf, f, 16)

    for r in (2, 1, 3):
        dr = (d + r) % 4
        i_out[r] = terms[pl.ds(pl.multiple_of(dr * CHUNK, CHUNK), CHUNK)].astype(BF16)
        start(i_out.at[r], i_in.at[r], ("ix", r), x_dev(r))

    from_plane(row_buf, 0)
    total = row_buf[0]
    for j in range(1, 16):
        total = total + row_buf[j]
    row_new = DECAY * row_mom[...] + (1.0 - DECAY) * total / HID
    row_out[...] = row_new
    rcol = jnp.broadcast_to(lax.rsqrt(row_new), (128, ROWS)).T
    rcol_out[...] = rcol
    row_acc[...] = rcol * rcol
    from_fsdp(col_buf, 16)
    total = col_buf[0]
    for j in range(1, 16):
        total = total + col_buf[j]
    col_new = DECAY * col_mom[...] + (1.0 - DECAY) * total / D
    col_out[...] = col_new

    def weigh(b, carry):
        rows = pl.ds(pl.multiple_of(b * 64, 64), 64)
        acc = jnp.zeros((64, 128), F32)
        for g in range(GROUPS):
            inverse = 1.0 / col_out[g]
            piece = grad[g, rows]
            piece = piece * piece * inverse
            acc = acc + piece[:, :128] + piece[:, 128:]
        return carry + jnp.sum(acc * row_acc[rows], axis=0, keepdims=True)

    u_lanes = lax.fori_loop(0, 8, weigh, jnp.zeros((1, 128), F32))
    a_lanes = (row_new[:, :128] + row_new[:, 128:256]) + (row_new[:, 256:384] + row_new[:, 384:])
    one_buf[f, :, :128] = u_lanes
    one_buf[f, :, 128:] = a_lanes
    to_fsdp(one_buf, f, 32)
    from_fsdp(one_buf, 32)
    total = one_buf[0]
    for j in range(1, 16):
        total = total + one_buf[j]
    two_buf[me] = total
    to_plane(two_buf, me, 48)

    acc = terms[pl.ds(pl.multiple_of(d * CHUNK, CHUNK), CHUNK)]
    for r in (1, 3, 2):
        wait(i_in.at[r], ("ix", r))
        acc = acc + i_in[r].astype(F32)
    i_sum[...] = acc
    for r in (1, 3, 2):
        mr = (m + r) % 4
        j_out[r] = i_sum[:, pl.ds(pl.multiple_of(mr * 128, 128), 128)].astype(BF16)
        start(j_out.at[r], j_in.at[r], ("jz", r), {"mp": mr})

    from_plane(two_buf, 48)
    total = two_buf[0]
    for j in range(1, 16):
        total = total + two_buf[j]
    scal_out[:, :128] = total[:, :128]
    scal_out[:, 128:] = two_buf[me][:, 128:]

    acc = i_sum[:, pl.ds(pl.multiple_of(m * 128, 128), 128)]
    for r in (1, 3, 2):
        wait(j_in.at[r], ("jz", r))
        acc = acc + j_in[r].astype(F32)
    inp_out[...] = acc.astype(BF16)

    for copy in sent:
        copy.wait_send()
    for copy in first:
        copy.wait()
    assert len(number.numbers) <= N_SEMS, len(number.numbers)


def last_kernel(grad, rcol, row_new, col_new, scal, inp, upd_out, row_out, col_out, inp_out, rms_out):
    total = jnp.sum(scal[:, :128], axis=1, keepdims=True)
    mean = jnp.sum(scal[:, 128:], axis=1, keepdims=True) / D
    rms = jnp.sqrt(mean * total / (D * HID))
    factor = jnp.sqrt(mean) / jnp.maximum(1.0, rms / clip_level)
    rows = grad.shape[1]
    left = rcol[...] * factor
    for g in range(GROUPS):
        right = lax.rsqrt(col_new[g])
        for h in (0, 1):
            lanes = slice(h * 128, h * 128 + 128)
            upd_out[pl.ds(2 * g + h, rows, stride=16), :] = grad[g, :, lanes] * left * right[:, lanes]

    @pl.when(pl.program_id(0) == 0)
    def _():
        row_out[...] = row_new[...]
        col_out[...] = col_new[...]
        inp_out[...] = inp[...]
        rms_out[...] = rms


def per_device(tokens_in, weight, cotangent, row_moment, col_moment):
    f = lax.axis_index("fsdp")
    c, y, zh = f % 2, (f // 2) % 4, f // 8
    upstream = lax.dynamic_slice(cotangent, (zh * HALF, 0, (c * 4 + y) * COLS), (HALF, 4, COLS))
    upstream = upstream.swapaxes(0, 1)
    vmem = pl.BlockSpec(memory_space=pltpu.VMEM)
    hbm = pl.BlockSpec(memory_space=pl.ANY)
    sds = jax.ShapeDtypeStruct
    grad, inp, row_new, rcol, col_new, scal = pl.pallas_call(
        main_kernel,
        name="main",
        out_shape=(
            sds((GROUPS, ROWS, COLS), F32),
            sds((CHUNK, 128), BF16),
            sds((1, ROWS), F32),
            sds((ROWS, 128), F32),
            sds((GROUPS, 1, COLS), F32),
            sds((1, 256), F32),
        ),
        in_specs=[hbm, hbm, hbm, vmem, vmem],
        out_specs=(hbm, vmem, vmem, vmem, vmem, vmem),
        scratch_shapes=[
            pltpu.VMEM((4, CHUNK, ROWS), BF16),
            pltpu.VMEM((4, CHUNK, ROWS), BF16),
            pltpu.VMEM((ROWS, 4 * CHUNK), BF16),
            pltpu.VMEM((GROUPS, ROWS, COLS), BF16),
            pltpu.VMEM((4, ROWS, COLS), BF16),
            pltpu.VMEM((4, HALF, COLS), BF16),
            pltpu.VMEM((4, CHUNK, COLS), BF16),
            pltpu.VMEM((4, CHUNK, COLS), BF16),
            pltpu.VMEM((4, 2, CHUNK, COLS), BF16),
            pltpu.VMEM((4, CHUNK, COLS), BF16),
            pltpu.VMEM((4, CHUNK, COLS), BF16),
            pltpu.VMEM((4, CHUNK, COLS), F32),
            pltpu.VMEM((4, CHUNK, COLS), F32),
            pltpu.VMEM((4, HALF, COLS), BF16),
            pltpu.VMEM((4, HALF, COLS), BF16),
            pltpu.VMEM((GROUPS, 4 * CHUNK, COLS), BF16),
            pltpu.VMEM((GROUPS, ROWS, COLS), F32),
            pltpu.VMEM((4 * CHUNK, ROWS), F32),
            pltpu.VMEM((4, CHUNK, ROWS), BF16),
            pltpu.VMEM((4, CHUNK, ROWS), BF16),
            pltpu.VMEM((CHUNK, ROWS), F32),
            pltpu.VMEM((4, CHUNK, 128), BF16),
            pltpu.VMEM((4, CHUNK, 128), BF16),
            pltpu.VMEM((ROWS, 128), F32),
            pltpu.VMEM((16, 1, ROWS), F32),
            pltpu.VMEM((16, GROUPS, 1, COLS), F32),
            pltpu.VMEM((16, 1, 256), F32),
            pltpu.VMEM((16, 1, 256), F32),
            pltpu.SemaphoreType.DMA((N_SEMS,)),
            pltpu.SemaphoreType.DMA((N_SEMS,)),
            pltpu.SemaphoreType.DMA((18,)),
            pltpu.SemaphoreType.DMA((64,)),
            pltpu.SemaphoreType.DMA((64,)),
        ],
        compiler_params=pltpu.CompilerParams(
            collective_id=0, has_side_effects=True, vmem_limit_bytes=44 * 1024 * 1024
        ),
        cost_estimate=pl.CostEstimate(flops=3 * 2**30, bytes_accessed=8 * 2**20, transcendentals=2**16),
    )(
        tokens_in,
        weight.reshape(ROWS, GROUPS * COLS),
        upstream,
        row_moment.reshape(1, ROWS),
        col_moment.reshape(GROUPS, 1, COLS),
    )
    steps = 4
    rows = ROWS // steps
    whole = lambda *shape: pl.BlockSpec(shape, lambda i: (0,) * len(shape))
    update, row_new, col_new, input_grad, rms = pl.pallas_call(
        last_kernel,
        name="last",
        grid=(steps,),
        out_shape=(
            sds((ROWS * 16, 128), F32),
            sds((1, ROWS), F32),
            sds((GROUPS, 1, COLS), F32),
            sds((CHUNK, 128), BF16),
            sds((1, 1), F32),
        ),
        in_specs=[
            pl.BlockSpec((GROUPS, rows, COLS), lambda i: (0, i, 0)),
            pl.BlockSpec((rows, 128), lambda i: (i, 0)),
            whole(1, ROWS),
            whole(GROUPS, 1, COLS),
            whole(1, 256),
            whole(CHUNK, 128),
        ],
        out_specs=(
            pl.BlockSpec((rows * 16, 128), lambda i: (i, 0)),
            whole(1, ROWS),
            whole(GROUPS, 1, COLS),
            whole(CHUNK, 128),
            whole(1, 1),
        ),
        compiler_params=pltpu.CompilerParams(vmem_limit_bytes=44 * 1024 * 1024),
    )(grad, rcol, row_new, col_new, scal, inp)
    return (
        input_grad,
        row_new.reshape(ROWS),
        col_new.reshape(1, GROUPS * COLS),
        update.reshape(ROWS, 1, GROUPS * COLS),
        rms.reshape(()),
    )


def solution(mesh):
    in_specs = (
        P("dp", "fsdp"),
        P("fsdp", "dp", "mp"),
        P("dp", None, "mp"),
        P("fsdp"),
        P("dp", "mp"),
    )
    out_specs = (P("dp", ("fsdp", "mp")), P("fsdp"), P("dp", "mp"), P("fsdp", "dp", "mp"), P())
    return jax.shard_map(
        per_device, mesh=mesh, in_specs=in_specs, out_specs=out_specs, check_vma=False
    )
```

```python
import math

import jax
import jax.numpy as jnp
from jax import lax
from jax.experimental import pallas as pl
from jax.experimental.pallas import tpu as pltpu
from jax.sharding import PartitionSpec as P

MESH = pl.DeviceIdType.MESH
D = 8192
HID = 32768
STEP_INDEX = 10
DECAY = 1.0 - STEP_INDEX ** (-0.8)

tiny_term = 1e-30
clip_level = 1.0
gelu_coeff = 0.044715

F32 = jnp.float32
BF16 = jnp.bfloat16

CHUNK = 128
COLS = 256
ROWS = 512
GROUPS = 8
ORDER = (0, 1, 3, 2)
FIRST = ((0, 0), (0, 1), (3, 0), (1, 0), (3, 1), (1, 1))
LAST = ((2, 0), (2, 1))


def gelu_slope(values):
    root_term = math.sqrt(2.0 / math.pi)
    tanh_value = jnp.tanh(root_term * (values + gelu_coeff * values * values * values))
    return 0.5 * (1.0 + tanh_value) + 0.5 * values * (1.0 - tanh_value * tanh_value) * root_term * (
        1.0 + 3.0 * gelu_coeff * values * values
    )


class Slots:
    def __init__(self):
        self.numbers = {}

    def __call__(self, *key):
        return self.numbers.setdefault(key, len(self.numbers))


N_SEMS = 112


def main_kernel(
    tok, wgt, cot, row_mom, col_mom,
    grad, inp_out, row_out, rcol_out, col_out, scal_out,
    t_own, t_peer, t_tr, w_own, w_peer, c_raw, c_out, ct,
    so, rr, ho, zs, zr, sl, terms,
    i_out, i_in, i_sum, j_out, j_in, r_mom, c_mom,
    row_acc, row_buf, col_a, col_b, one_buf, two_buf,
    send, recv, local, peer_send, peer_recv,
):
    d, f, m = lax.axis_index("dp"), lax.axis_index("fsdp"), lax.axis_index("mp")
    c, y, zh = f % 2, (f // 2) % 4, f // 8
    fid = lambda zz, yy, cc: (zz * 4 + yy) * 2 + cc
    core_dev = {"fsdp": fid(zh, y, 1 - c)}
    z_dev = {"fsdp": fid(1 - zh, y, c)}
    y_dev = lambda rel: {"fsdp": fid(zh, (y + rel) % 4, c)}
    number = Slots()
    sent = []

    def start(src, dst, key, dev):
        i = number(*key)
        copy = pltpu.make_async_remote_copy(
            src_ref=src, dst_ref=dst, send_sem=send.at[i], recv_sem=recv.at[i],
            device_id=dev, device_id_type=MESH,
        )
        copy.start()
        sent.append(copy)

    def wait(dst, key):
        i = number(*key)
        pltpu.make_async_remote_copy(
            src_ref=dst, dst_ref=dst, send_sem=send.at[i], recv_sem=recv.at[i],
            device_id=core_dev, device_id_type=MESH,
        ).wait_recv()

    def x_dev(r):
        return {"dp": (d + r) % 4}

    g_own = c * 4 + y
    c_load = pltpu.make_async_copy(
        cot.at[:, :, pl.ds(pl.multiple_of(g_own * COLS, COLS), COLS)], c_raw, local.at[9]
    )
    c_load.start()
    t_load = pltpu.make_async_copy(tok, t_own.at[d], local.at[8])
    t_load.start()
    w_loads = {}
    for cc in (0, 1):
        for rel in (2, 3, 1, 0):
            g = (c if cc == 0 else 1 - c) * 4 + (y + rel) % 4
            copy = pltpu.make_async_copy(
                wgt.at[:, pl.ds(pl.multiple_of(g * COLS, COLS), COLS)], w_own.at[g],
                local.at[rel * 2 + cc],
            )
            copy.start()
            w_loads[rel, cc] = copy
    r_load = pltpu.make_async_copy(row_mom, r_mom, local.at[10])
    r_load.start()
    m_load = pltpu.make_async_copy(col_mom, c_mom, local.at[11])
    m_load.start()

    barrier = pltpu.get_barrier_semaphore()

    def greet(j, carry):
        pl.semaphore_signal(barrier, inc=1, device_id={"fsdp": (f + j) % 16}, device_id_type=MESH)
        pl.semaphore_signal(
            barrier, inc=1, device_id={"dp": (d + j // 4) % 4, "mp": (m + j % 4) % 4},
            device_id_type=MESH,
        )
        return carry

    lax.fori_loop(1, 16, greet, 0)
    c_load.wait()
    for b in range(4):
        c_out[b] = c_raw[:, b, :]
    pl.semaphore_wait(barrier, 30)

    for r in (1, 3, 2):
        start(tok, t_own.at[d], ("tok", r), x_dev(r))
    start(tok, t_peer.at[d], ("tpeer", 0), core_dev)
    for rel in (2, 3, 1, 0):
        yy = (y + rel) % 4
        g = (1 - c) * 4 + yy
        start(
            wgt.at[:, pl.ds(pl.multiple_of(g * COLS, COLS), COLS)], w_peer.at[yy],
            ("w", rel), core_dev,
        )
    for r in (1, 3, 2):
        start(c_out.at[(d + r) % 4], ct.at[d], ("ct", r), x_dev(r))

    have_w = set()

    def product(k, rel):
        dk, yy = (d + k) % 4, (y + rel) % 4
        if rel not in have_w:
            have_w.add(rel)
            w_loads[rel, 0].wait()
            wait(w_peer.at[yy], ("w", rel))
        return jnp.dot(
            t_own[dk], w_own[c * 4 + yy], preferred_element_type=F32
        ) + jnp.dot(t_peer[dk], w_peer[yy], preferred_element_type=F32)

    def stage_tokens(k):
        dk = (d + k) % 4
        if k == 0:
            t_load.wait()
        else:
            wait(t_own.at[dk], ("tok", 4 - k))
            start(t_own.at[dk], t_peer.at[dk], ("tpeer", k), core_dev)

    def stage_products(k):
        dk = (d + k) % 4
        wait(t_peer.at[dk], ("tpeer", k))
        for rel in (2, 1, 3):
            so[k, rel - 1] = product(k, rel).astype(BF16)
            start(so.at[k, rel - 1], rr.at[k, rel - 1], ("rs", k, rel), y_dev(rel))
        ho[k] = product(k, 0)

    def stage_sum(k):
        total = ho[k]
        for rel in (1, 3, 2):
            wait(rr.at[k, rel - 1], ("rs", k, rel))
            total = total + rr[k, rel - 1].astype(F32)
        ho[k] = total
        zs[k] = total.astype(BF16)
        start(zs.at[k], zr.at[k], ("z", k), z_dev)

    def chunk_of(k):
        dk = (d + k) % 4
        return pl.ds(pl.multiple_of(dk * CHUNK, CHUNK), CHUNK)

    def stage_slope(k):
        dk = (d + k) % 4
        if k == 0:
            upstream = c_out[d]
        else:
            wait(ct.at[dk], ("ct", 4 - k))
            upstream = ct[dk]
        wait(zr.at[k], ("z", k))
        hidden = ho[k] + zr[k].astype(F32)
        sl[g_own, chunk_of(k)] = (upstream.astype(F32) * gelu_slope(hidden)).astype(BF16)
        block = sl.at[g_own, chunk_of(k)]
        for rel in (2, 1, 3):
            start(block, block, ("ag", rel, k), y_dev(rel))
        start(block, block, ("core", 0, k), core_dev)

    def stage_arrive(k):
        for rel in (1, 3, 2):
            block = sl.at[c * 4 + (y + 4 - rel) % 4, chunk_of(k)]
            wait(block, ("ag", rel, k))
            start(block, block, ("core", 4 - rel, k), core_dev)

    def group_at(rel, cc):
        return (c if cc == 0 else 1 - c) * 4 + (y + rel) % 4

    def group(rel, cc, sums):
        g = group_at(rel, cc)
        if cc == 1:
            for k in ORDER:
                wait(sl.at[g, chunk_of(k)], ("core", rel, k))
        value = jnp.dot(t_tr[...], sl[g], preferred_element_type=F32)
        grad[g] = value
        squares = value * value + tiny_term
        sums[...] = jnp.sum(squares, axis=0, keepdims=True)
        lanes = squares[:, :128] + squares[:, 128:]
        if (rel, cc) == (0, 0):
            row_acc[...] = lanes
        else:
            row_acc[...] += lanes

    def group_terms(rel, cc):
        g = group_at(rel, cc)
        if cc == 1:
            w_loads[rel, 1].wait()
        part = lax.dot_general(
            sl[g], w_own[g], (((1,), (1,)), ((), ())), preferred_element_type=F32
        )
        if (rel, cc) == (0, 0):
            terms[...] = part
        else:
            terms[...] += part

    def to_fsdp(buf, slot, base):
        def one(j, carry):
            pltpu.make_async_remote_copy(
                src_ref=buf.at[slot], dst_ref=buf.at[slot], send_sem=peer_send.at[base + j],
                recv_sem=peer_recv.at[base + j], device_id={"fsdp": (f + j) % 16},
                device_id_type=MESH,
            ).start()
            return carry

        lax.fori_loop(1, 16, one, 0)

    def from_fsdp(buf, base):
        def one(j, carry):
            came = (f + 16 - j) % 16
            pltpu.make_async_remote_copy(
                src_ref=buf.at[came], dst_ref=buf.at[came], send_sem=peer_send.at[base + j],
                recv_sem=peer_recv.at[base + j], device_id={"fsdp": (f + j) % 16},
                device_id_type=MESH,
            ).wait()
            return carry

        lax.fori_loop(1, 16, one, 0)

    def to_plane(buf, slot, base):
        def one(j, carry):
            pltpu.make_async_remote_copy(
                src_ref=buf.at[slot], dst_ref=buf.at[slot], send_sem=peer_send.at[base + j],
                recv_sem=peer_recv.at[base + j],
                device_id={"dp": (d + j // 4) % 4, "mp": (m + j % 4) % 4},
                device_id_type=MESH,
            ).start()
            return carry

        lax.fori_loop(1, 16, one, 0)

    def from_plane(buf, base):
        def one(j, carry):
            came = ((d + 4 - j // 4) % 4) * 4 + (m + 4 - j % 4) % 4
            pltpu.make_async_remote_copy(
                src_ref=buf.at[came], dst_ref=buf.at[came], send_sem=peer_send.at[base + j],
                recv_sem=peer_recv.at[base + j],
                device_id={"dp": (d + j // 4) % 4, "mp": (m + j % 4) % 4},
                device_id_type=MESH,
            ).wait()
            return carry

        lax.fori_loop(1, 16, one, 0)

    stage_tokens(0)
    stage_products(0)
    stage_tokens(1)
    stage_tokens(3)
    stage_products(1)
    stage_products(3)
    stage_sum(0)
    stage_tokens(2)
    stage_products(2)
    stage_sum(1)
    for k in ORDER:
        dk = (d + k) % 4
        t_tr[:, pl.ds(pl.multiple_of(dk * CHUNK, CHUNK), CHUNK)] = t_own[dk].T
    stage_slope(0)
    stage_sum(3)
    stage_sum(2)
    stage_slope(1)
    stage_slope(3)
    stage_arrive(0)
    stage_slope(2)
    group(0, 0, col_a.at[f, 0])
    group_terms(0, 0)
    stage_arrive(1)
    stage_arrive(3)
    group(0, 1, col_a.at[f, 1])
    stage_arrive(2)
    for i in range(2, 6):
        group(*FIRST[i], col_a.at[f, i])
    to_fsdp(col_a, f, 16)
    for i in range(2):
        group(*LAST[i], col_b.at[f, i])
    to_fsdp(col_b, f, 64)

    me = d * 4 + m
    row_buf[me] = jnp.sum(row_acc[...].T, axis=0, keepdims=True)

    to_plane(row_buf, me, 0)
    for i in range(1, 6):
        group_terms(*FIRST[i])
    for i in range(2):
        group_terms(*LAST[i])

    for r in (2, 1, 3):
        dr = (d + r) % 4
        i_out[r] = terms[pl.ds(pl.multiple_of(dr * CHUNK, CHUNK), CHUNK)].astype(BF16)
        start(i_out.at[r], i_in.at[r], ("ix", r), x_dev(r))

    from_plane(row_buf, 0)
    total = row_buf[0]
    for j in range(1, 16):
        total = total + row_buf[j]
    r_load.wait()
    row_new = DECAY * r_mom[...] + (1.0 - DECAY) * total / HID
    row_out[...] = row_new
    rcol = jnp.broadcast_to(lax.rsqrt(row_new), (128, ROWS)).T
    rcol_out[...] = rcol
    row_acc[...] = rcol * rcol
    from_fsdp(col_a, 16)
    m_load.wait()

    def col_finish(own_core, yy):
        g = own_core * 4 + yy
        total = jnp.zeros((1, COLS), F32)
        for s in range(16):
            place = ((yy - s // 2) % 4, own_core ^ (s % 2))
            if place in FIRST:
                total = total + col_a[s, FIRST.index(place)]
            else:
                total = total + col_b[s, LAST.index(place)]
        col_out[g] = DECAY * c_mom[g] + (1.0 - DECAY) * total / D

    from_fsdp(col_b, 64)
    for own_core in (0, 1):
        for yy in range(4):
            col_finish(own_core, yy)

    def weigh(b, carry):
        rows = pl.ds(pl.multiple_of(b * 64, 64), 64)
        acc = jnp.zeros((64, 128), F32)
        for g in range(GROUPS):
            inverse = 1.0 / col_out[g]
            piece = grad[g, rows]
            piece = piece * piece * inverse
            acc = acc + piece[:, :128] + piece[:, 128:]
        return carry + jnp.sum(acc * row_acc[rows], axis=0, keepdims=True)

    u_lanes = lax.fori_loop(0, 8, weigh, jnp.zeros((1, 128), F32))
    a_lanes = (row_new[:, :128] + row_new[:, 128:256]) + (row_new[:, 256:384] + row_new[:, 384:])
    one_buf[f, :, :128] = u_lanes
    one_buf[f, :, 128:] = a_lanes
    to_fsdp(one_buf, f, 32)
    from_fsdp(one_buf, 32)
    total = one_buf[0]
    for j in range(1, 16):
        total = total + one_buf[j]
    two_buf[me] = total
    to_plane(two_buf, me, 48)

    acc = terms[pl.ds(pl.multiple_of(d * CHUNK, CHUNK), CHUNK)]
    for r in (1, 3, 2):
        wait(i_in.at[r], ("ix", r))
        acc = acc + i_in[r].astype(F32)
    i_sum[...] = acc
    for r in (1, 3, 2):
        mr = (m + r) % 4
        j_out[r] = i_sum[:, pl.ds(pl.multiple_of(mr * 128, 128), 128)].astype(BF16)
        start(j_out.at[r], j_in.at[r], ("jz", r), {"mp": mr})

    from_plane(two_buf, 48)
    total = two_buf[0]
    for j in range(1, 16):
        total = total + two_buf[j]
    scal_out[:, :128] = total[:, :128]
    scal_out[:, 128:] = two_buf[me][:, 128:]

    acc = i_sum[:, pl.ds(pl.multiple_of(m * 128, 128), 128)]
    for r in (1, 3, 2):
        wait(j_in.at[r], ("jz", r))
        acc = acc + j_in[r].astype(F32)
    inp_out[...] = acc.astype(BF16)

    for copy in sent:
        copy.wait_send()
    assert len(number.numbers) <= N_SEMS, len(number.numbers)


def last_kernel(grad, rcol, row_new, col_new, scal, inp, upd_out, row_out, col_out, inp_out, rms_out):
    total = jnp.sum(scal[:, :128], axis=1, keepdims=True)
    mean = jnp.sum(scal[:, 128:], axis=1, keepdims=True) / D
    rms = jnp.sqrt(mean * total / (D * HID))
    factor = jnp.sqrt(mean) / jnp.maximum(1.0, rms / clip_level)
    rows = upd_out.shape[0] // 16
    here = pl.ds(pl.multiple_of(pl.program_id(0) * rows, rows), rows)
    left = rcol[here] * factor
    for g in range(GROUPS):
        right = lax.rsqrt(col_new[g])
        for h in (0, 1):
            lanes = slice(h * 128, h * 128 + 128)
            upd_out[pl.ds(2 * g + h, rows, stride=16), :] = grad[g, here, lanes] * left * right[:, lanes]

    @pl.when(pl.program_id(0) == 0)
    def _():
        row_out[...] = row_new[...]
        col_out[...] = col_new[...]
        inp_out[...] = inp[...]
        rms_out[...] = rms


def per_device(tokens_in, weight, cotangent, row_moment, col_moment):
    vmem = pl.BlockSpec(memory_space=pltpu.VMEM)
    hbm = pl.BlockSpec(memory_space=pltpu.HBM)
    sds = jax.ShapeDtypeStruct
    grad, inp, row_new, rcol, col_new, scal = pl.pallas_call(
        main_kernel,
        name="main",
        out_shape=(
            sds((GROUPS, ROWS, COLS), F32),
            sds((CHUNK, 128), BF16),
            sds((1, ROWS), F32),
            sds((ROWS, 128), F32),
            sds((GROUPS, 1, COLS), F32),
            sds((1, 256), F32),
        ),
        in_specs=[hbm] * 5,
        out_specs=(vmem, vmem, vmem, vmem, vmem, vmem),
        scratch_shapes=[
            pltpu.VMEM((4, CHUNK, ROWS), BF16),
            pltpu.VMEM((4, CHUNK, ROWS), BF16),
            pltpu.VMEM((ROWS, 4 * CHUNK), BF16),
            pltpu.VMEM((GROUPS, ROWS, COLS), BF16),
            pltpu.VMEM((4, ROWS, COLS), BF16),
            pltpu.VMEM((CHUNK, 4, COLS), BF16),
            pltpu.VMEM((4, CHUNK, COLS), BF16),
            pltpu.VMEM((4, CHUNK, COLS), BF16),
            pltpu.VMEM((4, 3, CHUNK, COLS), BF16),
            pltpu.VMEM((4, 3, CHUNK, COLS), BF16),
            pltpu.VMEM((4, CHUNK, COLS), F32),
            pltpu.VMEM((4, CHUNK, COLS), BF16),
            pltpu.VMEM((4, CHUNK, COLS), BF16),
            pltpu.VMEM((GROUPS, 4 * CHUNK, COLS), BF16),
            pltpu.VMEM((4 * CHUNK, ROWS), F32),
            pltpu.VMEM((4, CHUNK, ROWS), BF16),
            pltpu.VMEM((4, CHUNK, ROWS), BF16),
            pltpu.VMEM((CHUNK, ROWS), F32),
            pltpu.VMEM((4, CHUNK, 128), BF16),
            pltpu.VMEM((4, CHUNK, 128), BF16),
            pltpu.VMEM((1, ROWS), F32),
            pltpu.VMEM((GROUPS, 1, COLS), F32),
            pltpu.VMEM((ROWS, 128), F32),
            pltpu.VMEM((16, 1, ROWS), F32),
            pltpu.VMEM((16, 6, 1, COLS), F32),
            pltpu.VMEM((16, 2, 1, COLS), F32),
            pltpu.VMEM((16, 1, 256), F32),
            pltpu.VMEM((16, 1, 256), F32),
            pltpu.SemaphoreType.DMA((N_SEMS,)),
            pltpu.SemaphoreType.DMA((N_SEMS,)),
            pltpu.SemaphoreType.DMA((12,)),
            pltpu.SemaphoreType.DMA((80,)),
            pltpu.SemaphoreType.DMA((80,)),
        ],
        compiler_params=pltpu.CompilerParams(
            collective_id=0, has_side_effects=True, vmem_limit_bytes=44 * 1024 * 1024
        ),
        cost_estimate=pl.CostEstimate(flops=3 * 2**30, bytes_accessed=8 * 2**20, transcendentals=2**16),
    )(
        tokens_in,
        weight.reshape(ROWS, GROUPS * COLS),
        cotangent,
        row_moment.reshape(1, ROWS),
        col_moment.reshape(GROUPS, 1, COLS),
    )
    steps = 4
    rows = ROWS // steps
    whole = lambda *shape: pl.BlockSpec(shape, lambda i: (0,) * len(shape))
    update, row_new, col_new, input_grad, rms = pl.pallas_call(
        last_kernel,
        name="last",
        grid=(steps,),
        out_shape=(
            sds((ROWS * 16, 128), F32),
            sds((1, ROWS), F32),
            sds((GROUPS, 1, COLS), F32),
            sds((CHUNK, 128), BF16),
            sds((1, 1), F32),
        ),
        in_specs=[
            vmem,
            vmem,
            whole(1, ROWS),
            whole(GROUPS, 1, COLS),
            whole(1, 256),
            whole(CHUNK, 128),
        ],
        out_specs=(
            pl.BlockSpec((rows * 16, 128), lambda i: (i, 0)),
            whole(1, ROWS),
            whole(GROUPS, 1, COLS),
            whole(CHUNK, 128),
            whole(1, 1),
        ),
        compiler_params=pltpu.CompilerParams(vmem_limit_bytes=44 * 1024 * 1024),
    )(grad, rcol, row_new, col_new, scal, inp)
    return (
        input_grad,
        row_new.reshape(ROWS),
        col_new.reshape(1, GROUPS * COLS),
        update.reshape(ROWS, 1, GROUPS * COLS),
        rms.reshape(()),
    )


def solution(mesh):
    in_specs = (
        P("dp", "fsdp"),
        P("fsdp", "dp", "mp"),
        P("dp", None, "mp"),
        P("fsdp"),
        P("dp", "mp"),
    )
    out_specs = (P("dp", ("fsdp", "mp")), P("fsdp"), P("dp", "mp"), P("fsdp", "dp", "mp"), P())
    return jax.shard_map(
        per_device, mesh=mesh, in_specs=in_specs, out_specs=out_specs, check_vma=False
    )
```

```python
import math

import jax
import jax.numpy as jnp
from jax import lax
from jax.experimental import pallas as pl
from jax.experimental.pallas import tpu as pltpu
from jax.sharding import PartitionSpec as P

MESH = pl.DeviceIdType.MESH
D = 8192
HID = 32768
STEP_INDEX = 10
DECAY = 1.0 - STEP_INDEX ** (-0.8)

tiny_term = 1e-30
clip_level = 1.0
gelu_coeff = 0.044715

F32 = jnp.float32
BF16 = jnp.bfloat16

CHUNK = 128
COLS = 256
ROWS = 512
GROUPS = 8
ORDER = (0, 1, 3, 2)
FIRST = ((0, 0), (0, 1), (3, 0), (1, 0), (3, 1), (1, 1))
LAST = ((2, 0), (2, 1))
FAR_FSDP = (8, 7, 9, 6, 10, 5, 11, 4, 12, 3, 13, 2, 14, 1, 15)
FAR_PLANE = (10, 9, 11, 8, 6, 14, 5, 7, 13, 15, 2, 1, 3, 4, 12)


def gelu_slope(values):
    root_term = math.sqrt(2.0 / math.pi)
    tanh_value = jnp.tanh(root_term * (values + gelu_coeff * values * values * values))
    return 0.5 * (1.0 + tanh_value) + 0.5 * values * (1.0 - tanh_value * tanh_value) * root_term * (
        1.0 + 3.0 * gelu_coeff * values * values
    )


class Slots:
    def __init__(self):
        self.numbers = {}

    def __call__(self, *key):
        return self.numbers.setdefault(key, len(self.numbers))


N_SEMS = 112


def main_kernel(
    tok, wgt, cot, row_mom, col_mom,
    shape_out, inp_out, row_out, col_out, scal_out,
    t_own, t_peer, t_tr, w_own, w_peer, c_raw, c_out, ct,
    so, rr, ho, zs, zr, sl, grad, shape, terms,
    i_out, i_in, i_sum, j_out, j_in, r_mom, c_mom,
    row_acc, row_buf, col_a, col_b, one_buf, two_buf,
    send, recv, local, peer_send, peer_recv, heard,
):
    d, f, m = lax.axis_index("dp"), lax.axis_index("fsdp"), lax.axis_index("mp")
    c, y, zh = f % 2, (f // 2) % 4, f // 8
    fid = lambda zz, yy, cc: (zz * 4 + yy) * 2 + cc
    core_dev = {"fsdp": fid(zh, y, 1 - c)}
    z_dev = {"fsdp": fid(1 - zh, y, c)}
    y_dev = lambda rel: {"fsdp": fid(zh, (y + rel) % 4, c)}
    number = Slots()
    sent = []

    def start(src, dst, key, dev):
        i = number(*key)
        copy = pltpu.make_async_remote_copy(
            src_ref=src, dst_ref=dst, send_sem=send.at[i], recv_sem=recv.at[i],
            device_id=dev, device_id_type=MESH,
        )
        copy.start()
        sent.append(copy)

    def wait(dst, key):
        i = number(*key)
        pltpu.make_async_remote_copy(
            src_ref=dst, dst_ref=dst, send_sem=send.at[i], recv_sem=recv.at[i],
            device_id=core_dev, device_id_type=MESH,
        ).wait_recv()

    def x_dev(r):
        return {"dp": (d + r) % 4}

    barrier = pltpu.get_barrier_semaphore()
    near = [core_dev, z_dev] + [y_dev(r) for r in (1, 3, 2)]
    near += [{"dp": (d + r) % 4} for r in (1, 3, 2)] + [{"mp": (m + r) % 4} for r in (1, 2, 3)]
    for dev in near:
        pl.semaphore_signal(barrier, inc=1, device_id=dev, device_id_type=MESH)

    g_own = c * 4 + y
    c_load = pltpu.make_async_copy(
        cot.at[:, :, pl.ds(pl.multiple_of(g_own * COLS, COLS), COLS)], c_raw, local.at[9]
    )
    c_load.start()
    t_load = pltpu.make_async_copy(tok, t_own.at[d], local.at[8])
    t_load.start()
    w_loads = {}
    for cc in (0, 1):
        for rel in (2, 3, 1, 0):
            g = (c if cc == 0 else 1 - c) * 4 + (y + rel) % 4
            copy = pltpu.make_async_copy(
                wgt.at[:, pl.ds(pl.multiple_of(g * COLS, COLS), COLS)], w_own.at[g],
                local.at[rel * 2 + cc],
            )
            copy.start()
            w_loads[rel, cc] = copy
    r_load = pltpu.make_async_copy(row_mom, r_mom, local.at[10])
    r_load.start()
    m_load = pltpu.make_async_copy(col_mom, c_mom, local.at[11])
    m_load.start()

    c_load.wait()
    for b in range(4):
        c_out[b] = c_raw[:, b, :]
    pl.semaphore_wait(barrier, len(near))

    for r in (1, 3, 2):
        start(tok, t_own.at[d], ("tok", r), x_dev(r))
    start(tok, t_peer.at[d], ("tpeer", 0), core_dev)
    for rel in (2, 3, 1, 0):
        yy = (y + rel) % 4
        g = (1 - c) * 4 + yy
        start(
            wgt.at[:, pl.ds(pl.multiple_of(g * COLS, COLS), COLS)], w_peer.at[yy],
            ("w", rel), core_dev,
        )
    for r in (1, 2, 3):
        pl.semaphore_signal(heard, inc=1, device_id={"mp": (m + r) % 4}, device_id_type=MESH)

    have_w = set()

    def product(k, rel):
        dk, yy = (d + k) % 4, (y + rel) % 4
        if rel not in have_w:
            have_w.add(rel)
            w_loads[rel, 0].wait()
            wait(w_peer.at[yy], ("w", rel))
        return jnp.dot(
            t_own[dk], w_own[c * 4 + yy], preferred_element_type=F32
        ) + jnp.dot(t_peer[dk], w_peer[yy], preferred_element_type=F32)

    def stage_tokens(k):
        dk = (d + k) % 4
        if k == 0:
            t_load.wait()
        else:
            wait(t_own.at[dk], ("tok", 4 - k))
            start(t_own.at[dk], t_peer.at[dk], ("tpeer", k), core_dev)

    def stage_products(k):
        dk = (d + k) % 4
        wait(t_peer.at[dk], ("tpeer", k))
        for rel in (2, 1, 3):
            so[k, rel - 1] = product(k, rel).astype(BF16)
            start(so.at[k, rel - 1], rr.at[k, rel - 1], ("rs", k, rel), y_dev(rel))
        ho[k] = product(k, 0)

    def stage_sum(k):
        total = ho[k]
        for rel in (1, 3, 2):
            wait(rr.at[k, rel - 1], ("rs", k, rel))
            total = total + rr[k, rel - 1].astype(F32)
        ho[k] = total
        zs[k] = total.astype(BF16)
        start(zs.at[k], zr.at[k], ("z", k), z_dev)

    def chunk_of(k):
        dk = (d + k) % 4
        return pl.ds(pl.multiple_of(dk * CHUNK, CHUNK), CHUNK)

    def stage_slope(k):
        dk = (d + k) % 4
        if k == 0:
            upstream = c_out[d]
        else:
            wait(ct.at[dk], ("ct", 4 - k))
            upstream = ct[dk]
        wait(zr.at[k], ("z", k))
        hidden = ho[k] + zr[k].astype(F32)
        sl[g_own, chunk_of(k)] = (upstream.astype(F32) * gelu_slope(hidden)).astype(BF16)
        block = sl.at[g_own, chunk_of(k)]
        for rel in (2, 1, 3):
            start(block, block, ("ag", rel, k), y_dev(rel))
        start(block, block, ("core", 0, k), core_dev)

    def stage_arrive(k):
        for rel in (1, 3, 2):
            block = sl.at[c * 4 + (y + 4 - rel) % 4, chunk_of(k)]
            wait(block, ("ag", rel, k))
            start(block, block, ("core", 4 - rel, k), core_dev)

    def group_at(rel, cc):
        return (c if cc == 0 else 1 - c) * 4 + (y + rel) % 4

    def group(rel, cc, sums):
        g = group_at(rel, cc)
        if cc == 1:
            for k in ORDER:
                wait(sl.at[g, chunk_of(k)], ("core", rel, k))
        value = jnp.dot(t_tr[...], sl[g], preferred_element_type=F32)
        grad[g] = value
        squares = value * value + tiny_term
        sums[...] = jnp.sum(squares, axis=0, keepdims=True)
        lanes = squares[:, :128] + squares[:, 128:]
        if (rel, cc) == (0, 0):
            row_acc[...] = lanes
        else:
            row_acc[...] += lanes

    def group_terms(rel, cc):
        g = group_at(rel, cc)
        if cc == 1:
            w_loads[rel, 1].wait()
        part = lax.dot_general(
            sl[g], w_own[g], (((1,), (1,)), ((), ())), preferred_element_type=F32
        )
        if (rel, cc) == (0, 0):
            terms[...] = part
        else:
            terms[...] += part

    late = []

    def peer_copy(buf, slot, base, j, dev):
        return pltpu.make_async_remote_copy(
            src_ref=buf.at[slot], dst_ref=buf.at[slot], send_sem=peer_send.at[base + j],
            recv_sem=peer_recv.at[base + j], device_id=dev, device_id_type=MESH,
        )

    def fsdp_dev(j):
        return {"fsdp": (f + j) % 16}

    def plane_dev(j):
        return {"dp": (d + j // 4) % 4, "mp": (m + j % 4) % 4}

    def to_fsdp(buf, slot, base):
        for j in FAR_FSDP:
            copy = peer_copy(buf, slot, base, j, fsdp_dev(j))
            copy.start()
            late.append(copy)

    def from_fsdp(buf, base):
        for j in FAR_FSDP[::-1]:
            peer_copy(buf, (f + 16 - j) % 16, base, j, fsdp_dev(j)).wait_recv()

    def to_plane(buf, slot, base):
        for j in FAR_PLANE:
            copy = peer_copy(buf, slot, base, j, plane_dev(j))
            copy.start()
            late.append(copy)

    def from_plane(buf, base):
        for j in FAR_PLANE[::-1]:
            came = ((d + 4 - j // 4) % 4) * 4 + (m + 4 - j % 4) % 4
            peer_copy(buf, came, base, j, plane_dev(j)).wait_recv()

    def transpose(k):
        dk = (d + k) % 4
        t_tr[:, pl.ds(pl.multiple_of(dk * CHUNK, CHUNK), CHUNK)] = t_own[dk].T

    stage_tokens(0)
    stage_products(0)
    stage_tokens(1)
    stage_tokens(3)
    stage_products(1)
    stage_products(3)
    stage_sum(0)
    stage_tokens(2)
    for r in (1, 3, 2):
        start(c_out.at[(d + r) % 4], ct.at[d], ("ct", r), x_dev(r))
    stage_products(2)
    stage_sum(1)
    for k in ORDER:
        transpose(k)
    stage_slope(0)
    stage_sum(3)
    stage_sum(2)
    stage_slope(1)
    stage_arrive(0)
    stage_slope(3)
    stage_arrive(1)
    stage_slope(2)
    group(0, 0, col_a.at[f, 0])
    group_terms(0, 0)
    stage_arrive(3)
    group(0, 1, col_a.at[f, 1])
    stage_arrive(2)
    for i in range(2, 6):
        group(*FIRST[i], col_a.at[f, i])
    to_fsdp(col_a, f, 16)
    for i in range(2):
        group(*LAST[i], col_b.at[f, i])
    to_fsdp(col_b, f, 64)

    me = d * 4 + m
    row_buf[me] = jnp.sum(row_acc[...].T, axis=0, keepdims=True)

    pl.semaphore_wait(heard, 3)
    to_plane(row_buf, me, 0)
    for i in range(1, 6):
        group_terms(*FIRST[i])
    for i in range(2):
        group_terms(*LAST[i])

    for r in (2, 1, 3):
        dr = (d + r) % 4
        i_out[r] = terms[pl.ds(pl.multiple_of(dr * CHUNK, CHUNK), CHUNK)].astype(BF16)
        start(i_out.at[r], i_in.at[r], ("ix", r), x_dev(r))

    from_plane(row_buf, 0)
    total = row_buf[0]
    for j in range(1, 16):
        total = total + row_buf[j]
    r_load.wait()
    row_new = DECAY * r_mom[...] + (1.0 - DECAY) * total / HID
    row_out[...] = row_new
    rcol = jnp.broadcast_to(lax.rsqrt(row_new), (128, ROWS)).T
    row_acc[...] = rcol
    from_fsdp(col_a, 16)
    m_load.wait()

    def col_finish(own_core, yy):
        g = own_core * 4 + yy
        total = jnp.zeros((1, COLS), F32)
        for s in range(16):
            place = ((yy - s // 2) % 4, own_core ^ (s % 2))
            if place in FIRST:
                total = total + col_a[s, FIRST.index(place)]
            else:
                total = total + col_b[s, LAST.index(place)]
        col_out[g] = DECAY * c_mom[g] + (1.0 - DECAY) * total / D

    from_fsdp(col_b, 64)
    for own_core in (0, 1):
        for yy in range(4):
            col_finish(own_core, yy)

    def weigh(b, carry):
        rows = pl.ds(pl.multiple_of(b * 64, 64), 64)
        acc = jnp.zeros((64, 128), F32)
        for g in range(GROUPS):
            inverse = 1.0 / col_out[g]
            piece = grad[g, rows]
            piece = piece * piece * inverse
            acc = acc + piece[:, :128] + piece[:, 128:]
        right = row_acc[rows]
        return carry + jnp.sum(acc * (right * right), axis=0, keepdims=True)

    u_lanes = lax.fori_loop(0, 8, weigh, jnp.zeros((1, 128), F32))
    a_lanes = (row_new[:, :128] + row_new[:, 128:256]) + (row_new[:, 256:384] + row_new[:, 384:])
    one_buf[f, :, :128] = u_lanes
    one_buf[f, :, 128:] = a_lanes
    to_fsdp(one_buf, f, 32)

    def spread_rows(b, carry):
        rows = pl.ds(pl.multiple_of(b * 64, 64), 64)
        left = row_acc[rows]
        for g in range(GROUPS):
            right = lax.rsqrt(col_out[g])
            for h in (0, 1):
                lanes = slice(h * 128, h * 128 + 128)
                shape[pl.ds(b * 1024 + 2 * g + h, 64, stride=16), :] = (
                    grad[g, rows, lanes] * left * right[:, lanes]
                )
        block = pl.ds(pl.multiple_of(b * 1024, 1024), 1024)
        pltpu.make_async_copy(shape.at[block], shape_out.at[block], peer_send.at[80 + b]).start()
        return carry

    lax.fori_loop(0, 8, spread_rows, 0)
    from_fsdp(one_buf, 32)
    total = one_buf[0]
    for j in range(1, 16):
        total = total + one_buf[j]
    two_buf[me] = total
    to_plane(two_buf, me, 48)

    acc = terms[pl.ds(pl.multiple_of(d * CHUNK, CHUNK), CHUNK)]
    for r in (1, 3, 2):
        wait(i_in.at[r], ("ix", r))
        acc = acc + i_in[r].astype(F32)
    i_sum[...] = acc
    for r in (1, 3, 2):
        mr = (m + r) % 4
        j_out[r] = i_sum[:, pl.ds(pl.multiple_of(mr * 128, 128), 128)].astype(BF16)
        start(j_out.at[r], j_in.at[r], ("jz", r), {"mp": mr})

    from_plane(two_buf, 48)
    total = two_buf[0]
    for j in range(1, 16):
        total = total + two_buf[j]
    scal_out[:, :128] = total[:, :128]
    scal_out[:, 128:] = two_buf[me][:, 128:]

    acc = i_sum[:, pl.ds(pl.multiple_of(m * 128, 128), 128)]
    for r in (1, 3, 2):
        wait(j_in.at[r], ("jz", r))
        acc = acc + j_in[r].astype(F32)
    inp_out[...] = acc.astype(BF16)

    def written(b, carry):
        block = pl.ds(pl.multiple_of(b * 1024, 1024), 1024)
        pltpu.make_async_copy(shape.at[block], shape_out.at[block], peer_send.at[80 + b]).wait()
        return carry

    lax.fori_loop(0, 8, written, 0)
    for copy in sent + late:
        copy.wait_send()
    assert len(number.numbers) <= N_SEMS, len(number.numbers)


def last_kernel(shape, row_new, col_new, scal, inp, upd_out, row_out, col_out, inp_out, rms_out):
    total = jnp.sum(scal[:, :128], axis=1, keepdims=True)
    mean = jnp.sum(scal[:, 128:], axis=1, keepdims=True) / D
    rms = jnp.sqrt(mean * total / (D * HID))
    factor = jnp.sqrt(mean) / jnp.maximum(1.0, rms / clip_level)
    upd_out[...] = shape[...] * factor

    @pl.when(pl.program_id(0) == 0)
    def _():
        row_out[...] = row_new[...]
        col_out[...] = col_new[...]
        inp_out[...] = inp[...]
        rms_out[...] = rms


def per_device(tokens_in, weight, cotangent, row_moment, col_moment):
    vmem = pl.BlockSpec(memory_space=pltpu.VMEM)
    hbm = pl.BlockSpec(memory_space=pltpu.HBM)
    sds = jax.ShapeDtypeStruct
    shape, inp, row_new, col_new, scal = pl.pallas_call(
        main_kernel,
        name="main",
        out_shape=(
            sds((ROWS * 16, 128), F32),
            sds((CHUNK, 128), BF16),
            sds((1, ROWS), F32),
            sds((GROUPS, 1, COLS), F32),
            sds((1, 256), F32),
        ),
        in_specs=[hbm] * 5,
        out_specs=(hbm, vmem, vmem, vmem, vmem),
        scratch_shapes=[
            pltpu.VMEM((4, CHUNK, ROWS), BF16),
            pltpu.VMEM((4, CHUNK, ROWS), BF16),
            pltpu.VMEM((ROWS, 4 * CHUNK), BF16),
            pltpu.VMEM((GROUPS, ROWS, COLS), BF16),
            pltpu.VMEM((4, ROWS, COLS), BF16),
            pltpu.VMEM((CHUNK, 4, COLS), BF16),
            pltpu.VMEM((4, CHUNK, COLS), BF16),
            pltpu.VMEM((4, CHUNK, COLS), BF16),
            pltpu.VMEM((4, 3, CHUNK, COLS), BF16),
            pltpu.VMEM((4, 3, CHUNK, COLS), BF16),
            pltpu.VMEM((4, CHUNK, COLS), F32),
            pltpu.VMEM((4, CHUNK, COLS), BF16),
            pltpu.VMEM((4, CHUNK, COLS), BF16),
            pltpu.VMEM((GROUPS, 4 * CHUNK, COLS), BF16),
            pltpu.VMEM((GROUPS, ROWS, COLS), F32),
            pltpu.VMEM((ROWS * 16, 128), F32),
            pltpu.VMEM((4 * CHUNK, ROWS), F32),
            pltpu.VMEM((4, CHUNK, ROWS), BF16),
            pltpu.VMEM((4, CHUNK, ROWS), BF16),
            pltpu.VMEM((CHUNK, ROWS), F32),
            pltpu.VMEM((4, CHUNK, 128), BF16),
            pltpu.VMEM((4, CHUNK, 128), BF16),
            pltpu.VMEM((1, ROWS), F32),
            pltpu.VMEM((GROUPS, 1, COLS), F32),
            pltpu.VMEM((ROWS, 128), F32),
            pltpu.VMEM((16, 1, ROWS), F32),
            pltpu.VMEM((16, 6, 1, COLS), F32),
            pltpu.VMEM((16, 2, 1, COLS), F32),
            pltpu.VMEM((16, 1, 256), F32),
            pltpu.VMEM((16, 1, 256), F32),
            pltpu.SemaphoreType.DMA((N_SEMS,)),
            pltpu.SemaphoreType.DMA((N_SEMS,)),
            pltpu.SemaphoreType.DMA((12,)),
            pltpu.SemaphoreType.DMA((88,)),
            pltpu.SemaphoreType.DMA((88,)),
            pltpu.SemaphoreType.REGULAR,
        ],
        compiler_params=pltpu.CompilerParams(
            collective_id=0, has_side_effects=True, vmem_limit_bytes=60 * 1024 * 1024
        ),
        cost_estimate=pl.CostEstimate(flops=3 * 2**30, bytes_accessed=8 * 2**20, transcendentals=2**16),
    )(
        tokens_in,
        weight.reshape(ROWS, GROUPS * COLS),
        cotangent,
        row_moment.reshape(1, ROWS),
        col_moment.reshape(GROUPS, 1, COLS),
    )
    steps = 2
    rows = ROWS // steps
    whole = lambda *shape: pl.BlockSpec(shape, lambda i: (0,) * len(shape))
    update, row_new, col_new, input_grad, rms = pl.pallas_call(
        last_kernel,
        name="last",
        grid=(steps,),
        out_shape=(
            sds((ROWS * 16, 128), F32),
            sds((1, ROWS), F32),
            sds((GROUPS, 1, COLS), F32),
            sds((CHUNK, 128), BF16),
            sds((1, 1), F32),
        ),
        in_specs=[
            pl.BlockSpec((rows * 16, 128), lambda i: (i, 0)),
            whole(1, ROWS),
            whole(GROUPS, 1, COLS),
            whole(1, 256),
            whole(CHUNK, 128),
        ],
        out_specs=(
            pl.BlockSpec((rows * 16, 128), lambda i: (i, 0)),
            whole(1, ROWS),
            whole(GROUPS, 1, COLS),
            whole(CHUNK, 128),
            whole(1, 1),
        ),
        compiler_params=pltpu.CompilerParams(vmem_limit_bytes=60 * 1024 * 1024),
    )(shape, row_new, col_new, scal, inp)
    return (
        input_grad,
        row_new.reshape(ROWS),
        col_new.reshape(1, GROUPS * COLS),
        update.reshape(ROWS, 1, GROUPS * COLS),
        rms.reshape(()),
    )


def solution(mesh):
    in_specs = (
        P("dp", "fsdp"),
        P("fsdp", "dp", "mp"),
        P("dp", None, "mp"),
        P("fsdp"),
        P("dp", "mp"),
    )
    out_specs = (P("dp", ("fsdp", "mp")), P("fsdp"), P("dp", "mp"), P("fsdp", "dp", "mp"), P())
    return jax.shard_map(
        per_device, mesh=mesh, in_specs=in_specs, out_specs=out_specs, check_vma=False
    )
```

```python
import math

import jax
import jax.numpy as jnp
from jax import lax
from jax.experimental import pallas as pl
from jax.experimental.pallas import tpu as pltpu
from jax.sharding import PartitionSpec as P

MESH = pl.DeviceIdType.MESH
D = 8192
HID = 32768
STEP_INDEX = 10
DECAY = 1.0 - STEP_INDEX ** (-0.8)

tiny_term = 1e-30
clip_level = 1.0
gelu_coeff = 0.044715

F32 = jnp.float32
BF16 = jnp.bfloat16

CHUNK = 128
COLS = 256
ROWS = 512
GROUPS = 8
ORDER = (0, 1, 3, 2)
FIRST = ((0, 0), (0, 1), (3, 0), (1, 0), (2, 0))
LAST = ((3, 1), (1, 1), (2, 1))
FAR_FSDP = (8, 7, 9, 6, 10, 5, 11, 4, 12, 3, 13, 2, 14, 1, 15)
FAR_CROSS = (10, 9, 11, 6, 14, 5, 7, 13, 15, 2, 8, 1, 3, 4, 12)
FAR_PLANE = (10, 9, 11, 8, 6, 14, 5, 7, 13, 15, 2, 1, 3, 4, 12)


def gelu_slope(values):
    root_term = math.sqrt(2.0 / math.pi)
    tanh_value = jnp.tanh(root_term * (values + gelu_coeff * values * values * values))
    return 0.5 * (1.0 + tanh_value) + 0.5 * values * (1.0 - tanh_value * tanh_value) * root_term * (
        1.0 + 3.0 * gelu_coeff * values * values
    )


class Slots:
    def __init__(self):
        self.numbers = {}

    def __call__(self, *key):
        return self.numbers.setdefault(key, len(self.numbers))


N_SEMS = 112


def main_kernel(
    tok, wgt, cot, row_mom, col_mom,
    shape_out, inp_out, row_out, col_out, scal_out,
    t_own, t_peer, t_tr, w_own, w_peer, c_raw, c_out, ct,
    so, rr, ho, zs, zr, sl, grad, shape,
    i_out, i_in, i_sum, j_out, j_in, r_mom, c_mom,
    row_acc, row_buf, col_a, col_b, one_buf, two_buf,
    send, recv, local, peer_send, peer_recv, heard,
):
    d, f, m = lax.axis_index("dp"), lax.axis_index("fsdp"), lax.axis_index("mp")
    c, y, zh = f % 2, (f // 2) % 4, f // 8
    fid = lambda zz, yy, cc: (zz * 4 + yy) * 2 + cc
    core_dev = {"fsdp": fid(zh, y, 1 - c)}
    z_dev = {"fsdp": fid(1 - zh, y, c)}
    y_dev = lambda rel: {"fsdp": fid(zh, (y + rel) % 4, c)}
    number = Slots()
    sent = []

    def start(src, dst, key, dev):
        i = number(*key)
        copy = pltpu.make_async_remote_copy(
            src_ref=src, dst_ref=dst, send_sem=send.at[i], recv_sem=recv.at[i],
            device_id=dev, device_id_type=MESH,
        )
        copy.start()
        sent.append(copy)

    def wait(dst, key):
        i = number(*key)
        pltpu.make_async_remote_copy(
            src_ref=dst, dst_ref=dst, send_sem=send.at[i], recv_sem=recv.at[i],
            device_id=core_dev, device_id_type=MESH,
        ).wait_recv()

    def x_dev(r):
        return {"dp": (d + r) % 4}

    barrier = pltpu.get_barrier_semaphore()
    near = [core_dev, z_dev] + [y_dev(r) for r in (1, 3, 2)]
    near += [{"dp": (d + r) % 4} for r in (1, 3, 2)] + [{"mp": (m + r) % 4} for r in (1, 2, 3)]
    for dev in near:
        pl.semaphore_signal(barrier, inc=1, device_id=dev, device_id_type=MESH)

    g_own = c * 4 + y
    t_load = pltpu.make_async_copy(tok, t_own.at[d], local.at[8])
    t_load.start()
    w_loads = {}

    def load_weight(cc):
        for rel in (2, 1, 3, 0):
            g = (c if cc == 0 else 1 - c) * 4 + (y + rel) % 4
            copy = pltpu.make_async_copy(
                wgt.at[:, pl.ds(pl.multiple_of(g * COLS, COLS), COLS)], w_own.at[g],
                local.at[rel * 2 + cc],
            )
            copy.start()
            w_loads[rel, cc] = copy

    load_weight(0)
    pl.semaphore_wait(barrier, len(near))

    for r in (1, 3, 2):
        start(tok, t_own.at[d], ("tok", r), x_dev(r))
    start(tok, t_peer.at[d], ("tpeer", 0), core_dev)
    for rel in (2, 1, 3, 0):
        yy = (y + rel) % 4
        g = (1 - c) * 4 + yy
        start(
            wgt.at[:, pl.ds(pl.multiple_of(g * COLS, COLS), COLS)], w_peer.at[yy],
            ("w", rel), core_dev,
        )
    c_load = pltpu.make_async_copy(
        cot.at[:, :, pl.ds(pl.multiple_of(g_own * COLS, COLS), COLS)], c_raw, local.at[9]
    )
    c_load.start()
    load_weight(1)
    r_load = pltpu.make_async_copy(row_mom, r_mom, local.at[10])
    r_load.start()
    m_load = pltpu.make_async_copy(col_mom, c_mom, local.at[11])
    m_load.start()
    for r in (1, 2, 3):
        pl.semaphore_signal(heard, inc=1, device_id={"mp": (m + r) % 4}, device_id_type=MESH)

    have_w = set()

    def product(k, rel):
        dk, yy = (d + k) % 4, (y + rel) % 4
        if rel not in have_w:
            have_w.add(rel)
            w_loads[rel, 0].wait()
            wait(w_peer.at[yy], ("w", rel))
        return jnp.dot(
            t_own[dk], w_own[c * 4 + yy], preferred_element_type=F32
        ) + jnp.dot(t_peer[dk], w_peer[yy], preferred_element_type=F32)

    def stage_tokens(k):
        dk = (d + k) % 4
        if k == 0:
            t_load.wait()
        else:
            wait(t_own.at[dk], ("tok", 4 - k))
            start(t_own.at[dk], t_peer.at[dk], ("tpeer", k), core_dev)

    def stage_products(k):
        dk = (d + k) % 4
        wait(t_peer.at[dk], ("tpeer", k))
        for rel in (2, 1, 3):
            so[k, rel - 1] = product(k, rel).astype(BF16)
            start(so.at[k, rel - 1], rr.at[k, rel - 1], ("rs", k, rel), y_dev(rel))
        ho[k] = product(k, 0)

    def stage_sum(k):
        total = ho[k]
        for rel in (1, 3, 2):
            wait(rr.at[k, rel - 1], ("rs", k, rel))
            total = total + rr[k, rel - 1].astype(F32)
        ho[k] = total
        zs[k] = total.astype(BF16)
        start(zs.at[k], zr.at[k], ("z", k), z_dev)

    def chunk_of(k):
        dk = (d + k) % 4
        return pl.ds(pl.multiple_of(dk * CHUNK, CHUNK), CHUNK)

    def stage_slope(k):
        dk = (d + k) % 4
        if k == 0:
            upstream = c_out[d]
        else:
            wait(ct.at[dk], ("ct", 4 - k))
            upstream = ct[dk]
        wait(zr.at[k], ("z", k))
        hidden = ho[k] + zr[k].astype(F32)
        sl[g_own, chunk_of(k)] = (upstream.astype(F32) * gelu_slope(hidden)).astype(BF16)
        block = sl.at[g_own, chunk_of(k)]
        for rel in (2, 1, 3):
            start(block, block, ("ag", rel, k), y_dev(rel))
        start(block, block, ("core", 0, k), core_dev)

    def stage_arrive(k):
        for rel in (1, 3, 2):
            block = sl.at[c * 4 + (y + 4 - rel) % 4, chunk_of(k)]
            wait(block, ("ag", rel, k))
            start(block, block, ("core", 4 - rel, k), core_dev)

    def group_at(rel, cc):
        return (c if cc == 0 else 1 - c) * 4 + (y + rel) % 4

    def group(rel, cc, sums):
        g = group_at(rel, cc)
        value = jnp.dot(t_tr[...], sl[g], preferred_element_type=F32)
        grad[g] = value
        squares = value * value + tiny_term
        sums[...] = jnp.sum(squares, axis=0, keepdims=True)
        lanes = squares[:, :128] + squares[:, 128:]
        if (rel, cc) == (0, 0):
            row_acc[...] = lanes
        else:
            row_acc[...] += lanes

    def stage_core(k, rels):
        for rel in rels:
            wait(sl.at[group_at(rel, 1), chunk_of(k)], ("core", rel, k))

    def input_terms(k):
        if k == 0:
            for rel in range(4):
                w_loads[rel, 1].wait()
        part = None
        for g in range(GROUPS):
            more = lax.dot_general(
                sl[g, chunk_of(k)], w_own[g], (((1,), (1,)), ((), ())), preferred_element_type=F32
            )
            part = more if part is None else part + more
        if k == 0:
            i_sum[...] = part
        else:
            i_out[k] = part.astype(BF16)
            start(i_out.at[k], i_in.at[k], ("ix", k), x_dev(k))

    late = []

    def peer_copy(buf, slot, base, j, dev):
        return pltpu.make_async_remote_copy(
            src_ref=buf.at[slot], dst_ref=buf.at[slot], send_sem=peer_send.at[base + j],
            recv_sem=peer_recv.at[base + j], device_id=dev, device_id_type=MESH,
        )

    def fsdp_dev(j):
        return {"fsdp": (f + j) % 16}

    def plane_dev(j):
        return {"dp": (d + j // 4) % 4, "mp": (m + j % 4) % 4}

    def to_fsdp(buf, slot, base):
        for j in FAR_FSDP:
            copy = peer_copy(buf, slot, base, j, fsdp_dev(j))
            copy.start()
            late.append(copy)

    def from_fsdp(buf, base):
        for j in FAR_FSDP[::-1]:
            peer_copy(buf, (f + 16 - j) % 16, base, j, fsdp_dev(j)).wait_recv()

    def to_plane(buf, slot, base):
        for j in FAR_PLANE:
            copy = peer_copy(buf, slot, base, j, plane_dev(j))
            copy.start()
            late.append(copy)

    z8 = (zh * 4 + m) * 2 + c

    def cross_dev(j):
        return {"dp": (d + j // 4) % 4, "fsdp": fid(zh, (y + j % 4) % 4, c)}

    def to_cross(buf, slot, base):
        for j in FAR_CROSS:
            copy = peer_copy(buf, slot, base, j, cross_dev(j))
            copy.start()
            late.append(copy)

    def from_cross(buf, base):
        for j in FAR_CROSS[::-1]:
            came = ((d + 4 - j // 4) % 4) * 4 + (y + 4 - j % 4) % 4
            peer_copy(buf, came, base, j, cross_dev(j)).wait_recv()

    def pole_dev(j):
        k = (z8 + j) % 16
        return {"fsdp": fid(k // 8, y, k % 2), "mp": (k // 2) % 4}

    def to_pole(buf, slot, base):
        for j in FAR_FSDP:
            copy = peer_copy(buf, slot, base, j, pole_dev(j))
            copy.start()
            late.append(copy)

    def from_pole(buf, base):
        for j in FAR_FSDP[::-1]:
            peer_copy(buf, (z8 + 16 - j) % 16, base, j, pole_dev(j)).wait_recv()

    def from_plane(buf, base):
        for j in FAR_PLANE[::-1]:
            came = ((d + 4 - j // 4) % 4) * 4 + (m + 4 - j % 4) % 4
            peer_copy(buf, came, base, j, plane_dev(j)).wait_recv()

    def transpose(k):
        dk = (d + k) % 4
        t_tr[:, pl.ds(pl.multiple_of(dk * CHUNK, CHUNK), CHUNK)] = t_own[dk].T

    stage_tokens(0)
    stage_products(0)
    c_load.wait()
    for b in range(4):
        c_out[b] = c_raw[:, b, :]
    stage_tokens(1)
    stage_tokens(3)
    stage_products(1)
    stage_products(3)
    stage_sum(0)
    stage_tokens(2)
    for r in (1, 3, 2):
        start(c_out.at[(d + r) % 4], ct.at[d], ("ct", r), x_dev(r))
    stage_products(2)
    stage_sum(1)
    for k in ORDER:
        transpose(k)
    stage_slope(0)
    stage_sum(3)
    stage_sum(2)
    stage_slope(1)
    stage_arrive(0)
    stage_slope(3)
    stage_arrive(1)
    stage_slope(2)
    stage_core(0, (0, 1, 3, 2))
    input_terms(0)
    group(0, 0, col_a.at[f, 0])
    stage_arrive(3)
    stage_core(1, (0,))
    stage_core(3, (0,))
    stage_core(2, (0,))
    group(0, 1, col_a.at[f, 1])
    stage_arrive(2)
    for i in range(2, 5):
        group(*FIRST[i], col_a.at[f, i])
    to_fsdp(col_a, f, 16)
    for k in (1, 3, 2):
        stage_core(k, (1, 3, 2))
    for i in range(3):
        group(*LAST[i], col_b.at[f, i])
    to_fsdp(col_b, f, 64)

    me = d * 4 + m
    row_buf[me] = jnp.sum(row_acc[...].T, axis=0, keepdims=True)

    pl.semaphore_wait(heard, 3)
    to_plane(row_buf, me, 0)
    for k in (2, 1, 3):
        input_terms(k)
    from_plane(row_buf, 0)
    total = row_buf[0]
    for j in range(1, 16):
        total = total + row_buf[j]
    r_load.wait()
    row_new = DECAY * r_mom[...] + (1.0 - DECAY) * total / HID
    row_out[...] = row_new
    rcol = jnp.broadcast_to(lax.rsqrt(row_new), (128, ROWS)).T
    row_acc[...] = rcol
    from_fsdp(col_a, 16)
    m_load.wait()

    def col_finish(own_core, yy):
        g = own_core * 4 + yy
        total = jnp.zeros((1, COLS), F32)
        for s in range(16):
            place = ((yy - s // 2) % 4, own_core ^ (s % 2))
            if place in FIRST:
                total = total + col_a[s, FIRST.index(place)]
            else:
                total = total + col_b[s, LAST.index(place)]
        col_out[g] = DECAY * c_mom[g] + (1.0 - DECAY) * total / D

    from_fsdp(col_b, 64)
    for own_core in (0, 1):
        for yy in range(4):
            col_finish(own_core, yy)

    def weigh(b, carry):
        rows = pl.ds(pl.multiple_of(b * 64, 64), 64)
        acc = jnp.zeros((64, 128), F32)
        for g in range(GROUPS):
            inverse = 1.0 / col_out[g]
            piece = grad[g, rows]
            piece = piece * piece * inverse
            acc = acc + piece[:, :128] + piece[:, 128:]
        right = row_acc[rows]
        return carry + jnp.sum(acc * (right * right), axis=0, keepdims=True)

    u_lanes = lax.fori_loop(0, 8, weigh, jnp.zeros((1, 128), F32))
    a_lanes = (row_new[:, :128] + row_new[:, 128:256]) + (row_new[:, 256:384] + row_new[:, 384:])
    here = d * 4 + y
    one_buf[z8, :, :128] = u_lanes
    one_buf[z8, :, 128:] = a_lanes
    to_pole(one_buf, z8, 32)

    acc = i_sum[...]
    for r in (1, 3, 2):
        wait(i_in.at[r], ("ix", r))
        acc = acc + i_in[r].astype(F32)
    i_sum[...] = acc
    for r in (1, 3, 2):
        mr = (m + r) % 4
        j_out[r] = i_sum[:, pl.ds(pl.multiple_of(mr * 128, 128), 128)].astype(BF16)
        start(j_out.at[r], j_in.at[r], ("jz", r), {"mp": mr})

    def spread_rows(b, carry):
        rows = pl.ds(pl.multiple_of(b * 64, 64), 64)
        left = row_acc[rows]
        for g in range(GROUPS):
            right = lax.rsqrt(col_out[g])
            for h in (0, 1):
                lanes = slice(h * 128, h * 128 + 128)
                shape[pl.ds(b * 1024 + 2 * g + h, 64, stride=16), :] = (
                    grad[g, rows, lanes] * left * right[:, lanes]
                )
        block = pl.ds(pl.multiple_of(b * 1024, 1024), 1024)
        pltpu.make_async_copy(shape.at[block], shape_out.at[block], peer_send.at[80 + b]).start()
        return carry

    lax.fori_loop(0, 8, spread_rows, 0)
    from_pole(one_buf, 32)
    total = one_buf[0]
    for j in range(1, 16):
        total = total + one_buf[j]
    two_buf[here] = total
    to_cross(two_buf, here, 48)

    from_cross(two_buf, 48)
    total = two_buf[0]
    for j in range(1, 16):
        total = total + two_buf[j]
    scal_out[...] = total

    acc = i_sum[:, pl.ds(pl.multiple_of(m * 128, 128), 128)]
    for r in (1, 3, 2):
        wait(j_in.at[r], ("jz", r))
        acc = acc + j_in[r].astype(F32)
    inp_out[...] = acc.astype(BF16)

    def written(b, carry):
        block = pl.ds(pl.multiple_of(b * 1024, 1024), 1024)
        pltpu.make_async_copy(shape.at[block], shape_out.at[block], peer_send.at[80 + b]).wait()
        return carry

    lax.fori_loop(0, 8, written, 0)
    for copy in sent + late:
        copy.wait_send()
    assert len(number.numbers) <= N_SEMS, len(number.numbers)


def last_kernel(shape, row_new, col_new, scal, inp, upd_out, row_out, col_out, inp_out, rms_out):
    total = jnp.sum(scal[:, :128], axis=1, keepdims=True)
    mean = jnp.sum(scal[:, 128:], axis=1, keepdims=True) / (16.0 * D)
    rms = jnp.sqrt(mean * total / (D * HID))
    factor = jnp.sqrt(mean) / jnp.maximum(1.0, rms / clip_level)
    upd_out[...] = shape[...] * factor

    @pl.when(pl.program_id(0) == 0)
    def _():
        row_out[...] = row_new[...]
        col_out[...] = col_new[...]
        inp_out[...] = inp[...]
        rms_out[...] = rms


def per_device(tokens_in, weight, cotangent, row_moment, col_moment):
    vmem = pl.BlockSpec(memory_space=pltpu.VMEM)
    hbm = pl.BlockSpec(memory_space=pltpu.HBM)
    sds = jax.ShapeDtypeStruct
    shape, inp, row_new, col_new, scal = pl.pallas_call(
        main_kernel,
        name="main",
        out_shape=(
            sds((ROWS * 16, 128), F32),
            sds((CHUNK, 128), BF16),
            sds((1, ROWS), F32),
            sds((GROUPS, 1, COLS), F32),
            sds((1, 256), F32),
        ),
        in_specs=[hbm] * 5,
        out_specs=(hbm, vmem, vmem, vmem, vmem),
        scratch_shapes=[
            pltpu.VMEM((4, CHUNK, ROWS), BF16),
            pltpu.VMEM((4, CHUNK, ROWS), BF16),
            pltpu.VMEM((ROWS, 4 * CHUNK), BF16),
            pltpu.VMEM((GROUPS, ROWS, COLS), BF16),
            pltpu.VMEM((4, ROWS, COLS), BF16),
            pltpu.VMEM((CHUNK, 4, COLS), BF16),
            pltpu.VMEM((4, CHUNK, COLS), BF16),
            pltpu.VMEM((4, CHUNK, COLS), BF16),
            pltpu.VMEM((4, 3, CHUNK, COLS), BF16),
            pltpu.VMEM((4, 3, CHUNK, COLS), BF16),
            pltpu.VMEM((4, CHUNK, COLS), F32),
            pltpu.VMEM((4, CHUNK, COLS), BF16),
            pltpu.VMEM((4, CHUNK, COLS), BF16),
            pltpu.VMEM((GROUPS, 4 * CHUNK, COLS), BF16),
            pltpu.VMEM((GROUPS, ROWS, COLS), F32),
            pltpu.VMEM((ROWS * 16, 128), F32),
            pltpu.VMEM((4, CHUNK, ROWS), BF16),
            pltpu.VMEM((4, CHUNK, ROWS), BF16),
            pltpu.VMEM((CHUNK, ROWS), F32),
            pltpu.VMEM((4, CHUNK, 128), BF16),
            pltpu.VMEM((4, CHUNK, 128), BF16),
            pltpu.VMEM((1, ROWS), F32),
            pltpu.VMEM((GROUPS, 1, COLS), F32),
            pltpu.VMEM((ROWS, 128), F32),
            pltpu.VMEM((16, 1, ROWS), F32),
            pltpu.VMEM((16, 5, 1, COLS), F32),
            pltpu.VMEM((16, 3, 1, COLS), F32),
            pltpu.VMEM((16, 1, 256), F32),
            pltpu.VMEM((16, 1, 256), F32),
            pltpu.SemaphoreType.DMA((N_SEMS,)),
            pltpu.SemaphoreType.DMA((N_SEMS,)),
            pltpu.SemaphoreType.DMA((12,)),
            pltpu.SemaphoreType.DMA((88,)),
            pltpu.SemaphoreType.DMA((88,)),
            pltpu.SemaphoreType.REGULAR,
        ],
        compiler_params=pltpu.CompilerParams(
            collective_id=0, has_side_effects=True, vmem_limit_bytes=60 * 1024 * 1024
        ),
        cost_estimate=pl.CostEstimate(flops=3 * 2**30, bytes_accessed=8 * 2**20, transcendentals=2**16),
    )(
        tokens_in,
        weight.reshape(ROWS, GROUPS * COLS),
        cotangent,
        row_moment.reshape(1, ROWS),
        col_moment.reshape(GROUPS, 1, COLS),
    )
    steps = 2
    rows = ROWS // steps
    whole = lambda *shape: pl.BlockSpec(shape, lambda i: (0,) * len(shape))
    update, row_new, col_new, input_grad, rms = pl.pallas_call(
        last_kernel,
        name="last",
        grid=(steps,),
        out_shape=(
            sds((ROWS * 16, 128), F32),
            sds((1, ROWS), F32),
            sds((GROUPS, 1, COLS), F32),
            sds((CHUNK, 128), BF16),
            sds((1, 1), F32),
        ),
        in_specs=[
            pl.BlockSpec((rows * 16, 128), lambda i: (i, 0)),
            whole(1, ROWS),
            whole(GROUPS, 1, COLS),
            whole(1, 256),
            whole(CHUNK, 128),
        ],
        out_specs=(
            pl.BlockSpec((rows * 16, 128), lambda i: (i, 0)),
            whole(1, ROWS),
            whole(GROUPS, 1, COLS),
            whole(CHUNK, 128),
            whole(1, 1),
        ),
        compiler_params=pltpu.CompilerParams(vmem_limit_bytes=60 * 1024 * 1024),
    )(shape, row_new, col_new, scal, inp)
    return (
        input_grad,
        row_new.reshape(ROWS),
        col_new.reshape(1, GROUPS * COLS),
        update.reshape(ROWS, 1, GROUPS * COLS),
        rms.reshape(()),
    )


def solution(mesh):
    in_specs = (
        P("dp", "fsdp"),
        P("fsdp", "dp", "mp"),
        P("dp", None, "mp"),
        P("fsdp"),
        P("dp", "mp"),
    )
    out_specs = (P("dp", ("fsdp", "mp")), P("fsdp"), P("dp", "mp"), P("fsdp", "dp", "mp"), P())
    return jax.shard_map(
        per_device, mesh=mesh, in_specs=in_specs, out_specs=out_specs, check_vma=False
    )
```

```python
import math

import jax
import jax.numpy as jnp
from jax import lax
from jax.experimental import pallas as pl
from jax.experimental.pallas import tpu as pltpu
from jax.sharding import PartitionSpec as P

MESH = pl.DeviceIdType.MESH
D = 8192
HID = 32768
STEP_INDEX = 10
DECAY = 1.0 - STEP_INDEX ** (-0.8)

tiny_term = 1e-30
clip_level = 1.0
gelu_coeff = 0.044715

F32 = jnp.float32
BF16 = jnp.bfloat16

CHUNK = 128
COLS = 256
ROWS = 512
GROUPS = 8
ORDER = (0, 1, 3, 2)
FIRST = ((0, 0), (0, 1), (3, 0), (1, 0), (2, 0))
LAST = ((3, 1), (1, 1), (2, 1))
FAR_FSDP = (8, 7, 9, 6, 10, 5, 11, 4, 12, 3, 13, 2, 14, 1, 15)
FAR_CROSS = (10, 9, 11, 6, 14, 5, 7, 13, 15, 2, 8, 1, 3, 4, 12)
FAR_PLANE = (10, 9, 11, 8, 6, 14, 5, 7, 13, 15, 2, 1, 3, 4, 12)


def gelu_slope(values):
    root_term = math.sqrt(2.0 / math.pi)
    tanh_value = jnp.tanh(root_term * (values + gelu_coeff * values * values * values))
    return 0.5 * (1.0 + tanh_value) + 0.5 * values * (1.0 - tanh_value * tanh_value) * root_term * (
        1.0 + 3.0 * gelu_coeff * values * values
    )


class Slots:
    def __init__(self):
        self.numbers = {}

    def __call__(self, *key):
        return self.numbers.setdefault(key, len(self.numbers))


N_SEMS = 112


def main_kernel(
    tok, wgt, cot, row_mom, col_mom,
    shape_out, inp_out, row_out, col_out, scal_out,
    t_own, t_peer, t_tr, w_own, w_peer, c_raw, c_out, ct,
    so, rr, ho, zs, zr, sl, grad, shape,
    i_out, i_in, i_sum, j_out, j_in, r_mom, c_mom,
    row_acc, row_buf, col_a, col_b, one_buf, two_buf,
    send, recv, local, peer_send, peer_recv, heard,
):
    d, f, m = lax.axis_index("dp"), lax.axis_index("fsdp"), lax.axis_index("mp")
    c, y, zh = f % 2, (f // 2) % 4, f // 8
    fid = lambda zz, yy, cc: (zz * 4 + yy) * 2 + cc
    core_dev = {"fsdp": fid(zh, y, 1 - c)}
    z_dev = {"fsdp": fid(1 - zh, y, c)}
    y_dev = lambda rel: {"fsdp": fid(zh, (y + rel) % 4, c)}
    number = Slots()
    sent = []

    def start(src, dst, key, dev):
        i = number(*key)
        copy = pltpu.make_async_remote_copy(
            src_ref=src, dst_ref=dst, send_sem=send.at[i], recv_sem=recv.at[i],
            device_id=dev, device_id_type=MESH,
        )
        copy.start()
        sent.append(copy)

    def wait(dst, key):
        i = number(*key)
        pltpu.make_async_remote_copy(
            src_ref=dst, dst_ref=dst, send_sem=send.at[i], recv_sem=recv.at[i],
            device_id=core_dev, device_id_type=MESH,
        ).wait_recv()

    def x_dev(r):
        return {"dp": (d + r) % 4}

    barrier = pltpu.get_barrier_semaphore()
    near = [core_dev, z_dev] + [y_dev(r) for r in (1, 3, 2)]
    near += [{"dp": (d + r) % 4} for r in (1, 3, 2)] + [{"mp": (m + r) % 4} for r in (1, 2, 3)]
    for dev in near:
        pl.semaphore_signal(barrier, inc=1, device_id=dev, device_id_type=MESH)

    g_own = c * 4 + y
    t_load = pltpu.make_async_copy(tok, t_own.at[d], local.at[8])
    t_load.start()
    w_loads = {}

    def load_weight(cc):
        for rel in (2, 1, 3, 0):
            g = (c if cc == 0 else 1 - c) * 4 + (y + rel) % 4
            copy = pltpu.make_async_copy(
                wgt.at[:, pl.ds(pl.multiple_of(g * COLS, COLS), COLS)], w_own.at[g],
                local.at[rel * 2 + cc],
            )
            copy.start()
            w_loads[rel, cc] = copy

    load_weight(0)
    pl.semaphore_wait(barrier, len(near))

    for r in (1, 3, 2):
        start(tok, t_own.at[d], ("tok", r), x_dev(r))
    start(tok, t_peer.at[d], ("tpeer", 0), core_dev)
    for rel in (2, 1, 3, 0):
        yy = (y + rel) % 4
        g = (1 - c) * 4 + yy
        start(
            wgt.at[:, pl.ds(pl.multiple_of(g * COLS, COLS), COLS)], w_peer.at[yy],
            ("w", rel), core_dev,
        )
    c_load = pltpu.make_async_copy(
        cot.at[:, :, pl.ds(pl.multiple_of(g_own * COLS, COLS), COLS)], c_raw, local.at[9]
    )
    c_load.start()
    load_weight(1)
    r_load = pltpu.make_async_copy(row_mom, r_mom, local.at[10])
    r_load.start()
    m_load = pltpu.make_async_copy(col_mom, c_mom, local.at[11])
    m_load.start()
    for r in (1, 2, 3):
        pl.semaphore_signal(heard, inc=1, device_id={"mp": (m + r) % 4}, device_id_type=MESH)

    have_w = set()

    def product(k, rel):
        dk, yy = (d + k) % 4, (y + rel) % 4
        if rel not in have_w:
            have_w.add(rel)
            w_loads[rel, 0].wait()
            wait(w_peer.at[yy], ("w", rel))
        return jnp.dot(
            t_own[dk], w_own[c * 4 + yy], preferred_element_type=F32
        ) + jnp.dot(t_peer[dk], w_peer[yy], preferred_element_type=F32)

    def stage_tokens(k):
        dk = (d + k) % 4
        if k == 0:
            t_load.wait()
        else:
            wait(t_own.at[dk], ("tok", 4 - k))
            start(t_own.at[dk], t_peer.at[dk], ("tpeer", k), core_dev)

    def stage_products(k):
        dk = (d + k) % 4
        wait(t_peer.at[dk], ("tpeer", k))
        for rel in (2, 1, 3):
            so[k, rel - 1] = product(k, rel).astype(BF16)
            start(so.at[k, rel - 1], rr.at[k, rel - 1], ("rs", k, rel), y_dev(rel))
        ho[k] = product(k, 0)

    def stage_sum(k):
        total = ho[k]
        for rel in (1, 3, 2):
            wait(rr.at[k, rel - 1], ("rs", k, rel))
            total = total + rr[k, rel - 1].astype(F32)
        ho[k] = total
        zs[k] = total.astype(BF16)
        start(zs.at[k], zr.at[k], ("z", k), z_dev)

    def chunk_of(k):
        dk = (d + k) % 4
        return pl.ds(pl.multiple_of(dk * CHUNK, CHUNK), CHUNK)

    def stage_slope(k):
        dk = (d + k) % 4
        if k == 0:
            upstream = c_out[d]
        else:
            wait(ct.at[dk], ("ct", 4 - k))
            upstream = ct[dk]
        wait(zr.at[k], ("z", k))
        hidden = ho[k] + zr[k].astype(F32)
        sl[g_own, chunk_of(k)] = (upstream.astype(F32) * gelu_slope(hidden)).astype(BF16)
        block = sl.at[g_own, chunk_of(k)]
        start(block, block, ("core", 0, k), core_dev)
        for rel in (2, 1, 3):
            start(block, block, ("ag", rel, k), y_dev(rel))

    def stage_arrive(k):
        for rel in (1, 3, 2):
            block = sl.at[c * 4 + (y + 4 - rel) % 4, chunk_of(k)]
            wait(block, ("ag", rel, k))
            start(block, block, ("core", 4 - rel, k), core_dev)

    def group_at(rel, cc):
        return (c if cc == 0 else 1 - c) * 4 + (y + rel) % 4

    def group(rel, cc, sums):
        g = group_at(rel, cc)
        value = jnp.dot(t_tr[...], sl[g], preferred_element_type=F32)
        grad[g] = value
        squares = value * value + tiny_term
        sums[...] = jnp.sum(squares, axis=0, keepdims=True)
        lanes = squares[:, :128] + squares[:, 128:]
        if (rel, cc) == (0, 0):
            row_acc[...] = lanes
        else:
            row_acc[...] += lanes

    def stage_core(k, rels):
        for rel in rels:
            wait(sl.at[group_at(rel, 1), chunk_of(k)], ("core", rel, k))

    def input_terms(k):
        if k == 0:
            for rel in range(4):
                w_loads[rel, 1].wait()
        part = None
        for g in range(GROUPS):
            more = lax.dot_general(
                sl[g, chunk_of(k)], w_own[g], (((1,), (1,)), ((), ())), preferred_element_type=F32
            )
            part = more if part is None else part + more
        if k == 0:
            i_sum[...] = part
        else:
            i_out[k] = part.astype(BF16)
            start(i_out.at[k], i_in.at[k], ("ix", k), x_dev(k))

    late = []

    def settle(copies):
        for copy in copies:
            copy.wait_send()
        copies.clear()

    def peer_copy(buf, slot, base, j, dev):
        return pltpu.make_async_remote_copy(
            src_ref=buf.at[slot], dst_ref=buf.at[slot], send_sem=peer_send.at[base + j],
            recv_sem=peer_recv.at[base + j], device_id=dev, device_id_type=MESH,
        )

    def fsdp_dev(j):
        return {"fsdp": (f + j) % 16}

    def plane_dev(j):
        return {"dp": (d + j // 4) % 4, "mp": (m + j % 4) % 4}

    def to_fsdp(buf, slot, base):
        for j in FAR_FSDP:
            copy = peer_copy(buf, slot, base, j, fsdp_dev(j))
            copy.start()
            late.append(copy)

    def from_fsdp(buf, base):
        for j in FAR_FSDP[::-1]:
            peer_copy(buf, (f + 16 - j) % 16, base, j, fsdp_dev(j)).wait_recv()

    def to_plane(buf, slot, base):
        for j in FAR_PLANE:
            copy = peer_copy(buf, slot, base, j, plane_dev(j))
            copy.start()
            late.append(copy)

    z8 = (zh * 4 + m) * 2 + c

    def cross_dev(j):
        return {"dp": (d + j // 4) % 4, "fsdp": fid(zh, (y + j % 4) % 4, c)}

    def to_cross(buf, slot, base):
        for j in FAR_CROSS:
            copy = peer_copy(buf, slot, base, j, cross_dev(j))
            copy.start()
            late.append(copy)

    def from_cross(buf, base):
        for j in FAR_CROSS[::-1]:
            came = ((d + 4 - j // 4) % 4) * 4 + (y + 4 - j % 4) % 4
            peer_copy(buf, came, base, j, cross_dev(j)).wait_recv()

    def pole_dev(j):
        k = (z8 + j) % 16
        return {"fsdp": fid(k // 8, y, k % 2), "mp": (k // 2) % 4}

    def to_pole(buf, slot, base):
        for j in FAR_FSDP:
            copy = peer_copy(buf, slot, base, j, pole_dev(j))
            copy.start()
            late.append(copy)

    def from_pole(buf, base):
        for j in FAR_FSDP[::-1]:
            peer_copy(buf, (z8 + 16 - j) % 16, base, j, pole_dev(j)).wait_recv()

    def from_plane(buf, base):
        for j in FAR_PLANE[::-1]:
            came = ((d + 4 - j // 4) % 4) * 4 + (m + 4 - j % 4) % 4
            peer_copy(buf, came, base, j, plane_dev(j)).wait_recv()

    def transpose(k):
        dk = (d + k) % 4
        t_tr[:, pl.ds(pl.multiple_of(dk * CHUNK, CHUNK), CHUNK)] = t_own[dk].T

    stage_tokens(0)
    stage_products(0)
    c_load.wait()
    for b in range(4):
        c_out[b] = c_raw[:, b, :]
    stage_tokens(1)
    stage_tokens(3)
    stage_products(1)
    stage_products(3)
    stage_sum(0)
    stage_tokens(2)
    for r in (1, 3, 2):
        start(c_out.at[(d + r) % 4], ct.at[d], ("ct", r), x_dev(r))
    stage_products(2)
    stage_sum(1)
    for k in ORDER:
        transpose(k)
    stage_slope(0)
    stage_sum(3)
    stage_sum(2)
    stage_slope(1)
    stage_arrive(0)
    stage_slope(3)
    stage_arrive(1)
    stage_slope(2)
    stage_core(0, (0, 1, 3, 2))
    input_terms(0)
    group(0, 0, col_a.at[f, 0])
    stage_arrive(3)
    stage_core(1, (0,))
    stage_core(3, (0,))
    stage_core(2, (0,))
    group(0, 1, col_a.at[f, 1])
    stage_arrive(2)
    for i in range(2, 5):
        group(*FIRST[i], col_a.at[f, i])
    to_fsdp(col_a, f, 16)
    for k in (1, 3, 2):
        stage_core(k, (1, 3, 2))
    for i in range(3):
        group(*LAST[i], col_b.at[f, i])
    to_fsdp(col_b, f, 64)

    sent_before = list(sent)
    sent.clear()
    me = d * 4 + m
    row_buf[me] = jnp.sum(row_acc[...].T, axis=0, keepdims=True)

    pl.semaphore_wait(heard, 3)
    to_plane(row_buf, me, 0)
    for k in (2, 1, 3):
        input_terms(k)
    settle(sent_before)
    from_plane(row_buf, 0)
    total = row_buf[0]
    for j in range(1, 16):
        total = total + row_buf[j]
    r_load.wait()
    row_new = DECAY * r_mom[...] + (1.0 - DECAY) * total / HID
    row_out[...] = row_new
    rcol = jnp.broadcast_to(lax.rsqrt(row_new), (128, ROWS)).T
    row_acc[...] = rcol
    from_fsdp(col_a, 16)
    m_load.wait()

    def col_finish(own_core, yy):
        g = own_core * 4 + yy
        total = jnp.zeros((1, COLS), F32)
        for s in range(16):
            place = ((yy - s // 2) % 4, own_core ^ (s % 2))
            if place in FIRST:
                total = total + col_a[s, FIRST.index(place)]
            else:
                total = total + col_b[s, LAST.index(place)]
        col_out[g] = DECAY * c_mom[g] + (1.0 - DECAY) * total / D

    from_fsdp(col_b, 64)
    for own_core in (0, 1):
        for yy in range(4):
            col_finish(own_core, yy)

    def weigh(b, carry):
        rows = pl.ds(pl.multiple_of(b * 64, 64), 64)
        acc = jnp.zeros((64, 128), F32)
        for g in range(GROUPS):
            inverse = 1.0 / col_out[g]
            piece = grad[g, rows]
            piece = piece * piece * inverse
            acc = acc + piece[:, :128] + piece[:, 128:]
        right = row_acc[rows]
        return carry + jnp.sum(acc * (right * right), axis=0, keepdims=True)

    u_lanes = lax.fori_loop(0, 8, weigh, jnp.zeros((1, 128), F32))
    a_lanes = (row_new[:, :128] + row_new[:, 128:256]) + (row_new[:, 256:384] + row_new[:, 384:])
    here = d * 4 + y
    one_buf[z8, :, :128] = u_lanes
    one_buf[z8, :, 128:] = a_lanes
    sums_before = list(late)
    late.clear()
    to_pole(one_buf, z8, 32)

    acc = i_sum[...]
    for r in (1, 3, 2):
        wait(i_in.at[r], ("ix", r))
        acc = acc + i_in[r].astype(F32)
    i_sum[...] = acc
    for r in (1, 3, 2):
        mr = (m + r) % 4
        j_out[r] = i_sum[:, pl.ds(pl.multiple_of(mr * 128, 128), 128)].astype(BF16)
        start(j_out.at[r], j_in.at[r], ("jz", r), {"mp": mr})

    def spread_rows(b, carry):
        rows = pl.ds(pl.multiple_of(b * 64, 64), 64)
        left = row_acc[rows]
        for g in range(GROUPS):
            right = lax.rsqrt(col_out[g])
            for h in (0, 1):
                lanes = slice(h * 128, h * 128 + 128)
                shape[pl.ds(b * 1024 + 2 * g + h, 64, stride=16), :] = (
                    grad[g, rows, lanes] * left * right[:, lanes]
                )
        block = pl.ds(pl.multiple_of(b * 1024, 1024), 1024)
        pltpu.make_async_copy(shape.at[block], shape_out.at[block], peer_send.at[80 + b]).start()
        return carry

    lax.fori_loop(0, 8, spread_rows, 0)
    settle(sums_before)
    from_pole(one_buf, 32)
    total = one_buf[0]
    for j in range(1, 16):
        total = total + one_buf[j]
    two_buf[here] = total
    pole_before = list(late)
    late.clear()
    to_cross(two_buf, here, 48)
    settle(pole_before)
    settle(sent)

    def written(b, carry):
        block = pl.ds(pl.multiple_of(b * 1024, 1024), 1024)
        pltpu.make_async_copy(shape.at[block], shape_out.at[block], peer_send.at[80 + b]).wait()
        return carry

    lax.fori_loop(0, 8, written, 0)
    from_cross(two_buf, 48)
    total = two_buf[0]
    for j in range(1, 16):
        total = total + two_buf[j]
    scal_out[...] = total

    acc = i_sum[:, pl.ds(pl.multiple_of(m * 128, 128), 128)]
    for r in (1, 3, 2):
        wait(j_in.at[r], ("jz", r))
        acc = acc + j_in[r].astype(F32)
    inp_out[...] = acc.astype(BF16)

    for copy in sent + late:
        copy.wait_send()
    assert len(number.numbers) <= N_SEMS, len(number.numbers)


def last_kernel(shape, row_new, col_new, scal, inp, upd_out, row_out, col_out, inp_out, rms_out):
    total = jnp.sum(scal[:, :128], axis=1, keepdims=True)
    mean = jnp.sum(scal[:, 128:], axis=1, keepdims=True) / (16.0 * D)
    rms = jnp.sqrt(mean * total / (D * HID))
    factor = jnp.sqrt(mean) / jnp.maximum(1.0, rms / clip_level)
    upd_out[...] = shape[...] * factor

    @pl.when(pl.program_id(0) == 0)
    def _():
        row_out[...] = row_new[...]
        col_out[...] = col_new[...]
        inp_out[...] = inp[...]
        rms_out[...] = rms


def per_device(tokens_in, weight, cotangent, row_moment, col_moment):
    vmem = pl.BlockSpec(memory_space=pltpu.VMEM)
    hbm = pl.BlockSpec(memory_space=pltpu.HBM)
    sds = jax.ShapeDtypeStruct
    shape, inp, row_new, col_new, scal = pl.pallas_call(
        main_kernel,
        name="main",
        out_shape=(
            sds((ROWS * 16, 128), F32),
            sds((CHUNK, 128), BF16),
            sds((1, ROWS), F32),
            sds((GROUPS, 1, COLS), F32),
            sds((1, 256), F32),
        ),
        in_specs=[hbm] * 5,
        out_specs=(hbm, vmem, vmem, vmem, vmem),
        scratch_shapes=[
            pltpu.VMEM((4, CHUNK, ROWS), BF16),
            pltpu.VMEM((4, CHUNK, ROWS), BF16),
            pltpu.VMEM((ROWS, 4 * CHUNK), BF16),
            pltpu.VMEM((GROUPS, ROWS, COLS), BF16),
            pltpu.VMEM((4, ROWS, COLS), BF16),
            pltpu.VMEM((CHUNK, 4, COLS), BF16),
            pltpu.VMEM((4, CHUNK, COLS), BF16),
            pltpu.VMEM((4, CHUNK, COLS), BF16),
            pltpu.VMEM((4, 3, CHUNK, COLS), BF16),
            pltpu.VMEM((4, 3, CHUNK, COLS), BF16),
            pltpu.VMEM((4, CHUNK, COLS), F32),
            pltpu.VMEM((4, CHUNK, COLS), BF16),
            pltpu.VMEM((4, CHUNK, COLS), BF16),
            pltpu.VMEM((GROUPS, 4 * CHUNK, COLS), BF16),
            pltpu.VMEM((GROUPS, ROWS, COLS), F32),
            pltpu.VMEM((ROWS * 16, 128), F32),
            pltpu.VMEM((4, CHUNK, ROWS), BF16),
            pltpu.VMEM((4, CHUNK, ROWS), BF16),
            pltpu.VMEM((CHUNK, ROWS), F32),
            pltpu.VMEM((4, CHUNK, 128), BF16),
            pltpu.VMEM((4, CHUNK, 128), BF16),
            pltpu.VMEM((1, ROWS), F32),
            pltpu.VMEM((GROUPS, 1, COLS), F32),
            pltpu.VMEM((ROWS, 128), F32),
            pltpu.VMEM((16, 1, ROWS), F32),
            pltpu.VMEM((16, 5, 1, COLS), F32),
            pltpu.VMEM((16, 3, 1, COLS), F32),
            pltpu.VMEM((16, 1, 256), F32),
            pltpu.VMEM((16, 1, 256), F32),
            pltpu.SemaphoreType.DMA((N_SEMS,)),
            pltpu.SemaphoreType.DMA((N_SEMS,)),
            pltpu.SemaphoreType.DMA((12,)),
            pltpu.SemaphoreType.DMA((88,)),
            pltpu.SemaphoreType.DMA((88,)),
            pltpu.SemaphoreType.REGULAR,
        ],
        compiler_params=pltpu.CompilerParams(
            collective_id=0, has_side_effects=True, vmem_limit_bytes=60 * 1024 * 1024
        ),
        cost_estimate=pl.CostEstimate(flops=3 * 2**30, bytes_accessed=8 * 2**20, transcendentals=2**16),
    )(
        tokens_in,
        weight.reshape(ROWS, GROUPS * COLS),
        cotangent,
        row_moment.reshape(1, ROWS),
        col_moment.reshape(GROUPS, 1, COLS),
    )
    steps = 2
    rows = ROWS // steps
    whole = lambda *shape: pl.BlockSpec(shape, lambda i: (0,) * len(shape))
    update, row_new, col_new, input_grad, rms = pl.pallas_call(
        last_kernel,
        name="last",
        grid=(steps,),
        out_shape=(
            sds((ROWS * 16, 128), F32),
            sds((1, ROWS), F32),
            sds((GROUPS, 1, COLS), F32),
            sds((CHUNK, 128), BF16),
            sds((1, 1), F32),
        ),
        in_specs=[
            pl.BlockSpec((rows * 16, 128), lambda i: (i, 0)),
            whole(1, ROWS),
            whole(GROUPS, 1, COLS),
            whole(1, 256),
            whole(CHUNK, 128),
        ],
        out_specs=(
            pl.BlockSpec((rows * 16, 128), lambda i: (i, 0)),
            whole(1, ROWS),
            whole(GROUPS, 1, COLS),
            whole(CHUNK, 128),
            whole(1, 1),
        ),
        compiler_params=pltpu.CompilerParams(vmem_limit_bytes=60 * 1024 * 1024),
    )(shape, row_new, col_new, scal, inp)
    return (
        input_grad,
        row_new.reshape(ROWS),
        col_new.reshape(1, GROUPS * COLS),
        update.reshape(ROWS, 1, GROUPS * COLS),
        rms.reshape(()),
    )


def solution(mesh):
    in_specs = (
        P("dp", "fsdp"),
        P("fsdp", "dp", "mp"),
        P("dp", None, "mp"),
        P("fsdp"),
        P("dp", "mp"),
    )
    out_specs = (P("dp", ("fsdp", "mp")), P("fsdp"), P("dp", "mp"), P("fsdp", "dp", "mp"), P())
    return jax.shard_map(
        per_device, mesh=mesh, in_specs=in_specs, out_specs=out_specs, check_vma=False
    )
```

```python
import math

import jax
import jax.numpy as jnp
from jax import lax
from jax.experimental import pallas as pl
from jax.experimental.pallas import tpu as pltpu
from jax.sharding import PartitionSpec as P

MESH = pl.DeviceIdType.MESH
D = 8192
HID = 32768
STEP_INDEX = 10
DECAY = 1.0 - STEP_INDEX ** (-0.8)

tiny_term = 1e-30
clip_level = 1.0
gelu_coeff = 0.044715

F32 = jnp.float32
BF16 = jnp.bfloat16

CHUNK = 128
COLS = 256
ROWS = 512
GROUPS = 8
ORDER = (0, 1, 3, 2)
FIRST = ((0, 0), (0, 1), (3, 0), (1, 0), (2, 0))
LAST = ((3, 1), (1, 1), (2, 1))
FAR_FSDP = (8, 7, 9, 6, 10, 5, 11, 4, 12, 3, 13, 2, 14, 1, 15)
FAR_CROSS = (10, 9, 11, 6, 14, 5, 7, 13, 15, 2, 8, 1, 3, 4, 12)
FAR_PLANE = (10, 9, 11, 8, 6, 14, 5, 7, 13, 15, 2, 1, 3, 4, 12)


def gelu_slope(values):
    root_term = math.sqrt(2.0 / math.pi)
    tanh_value = jnp.tanh(root_term * (values + gelu_coeff * values * values * values))
    return 0.5 * (1.0 + tanh_value) + 0.5 * values * (1.0 - tanh_value * tanh_value) * root_term * (
        1.0 + 3.0 * gelu_coeff * values * values
    )


class Slots:
    def __init__(self):
        self.numbers = {}

    def __call__(self, *key):
        return self.numbers.setdefault(key, len(self.numbers))


N_SEMS = 112


def main_kernel(
    tok, wgt, cot, row_mom, col_mom,
    shape_out, inp_out, row_out, col_out, scal_out,
    t_own, t_peer, t_tr, w_own, w_peer, c_raw, c_out, ct,
    so, rr, ho, zs, zr, sl, grad, shape,
    i_out, i_in, i_sum, j_out, j_in, r_mom, c_mom,
    row_acc, row_buf, col_a, col_b, one_buf, two_buf,
    send, recv, local, peer_send, peer_recv, heard,
):
    d, f, m = lax.axis_index("dp"), lax.axis_index("fsdp"), lax.axis_index("mp")
    c, y, zh = f % 2, (f // 2) % 4, f // 8
    fid = lambda zz, yy, cc: (zz * 4 + yy) * 2 + cc
    core_dev = {"fsdp": fid(zh, y, 1 - c)}
    z_dev = {"fsdp": fid(1 - zh, y, c)}
    y_dev = lambda rel: {"fsdp": fid(zh, (y + rel) % 4, c)}
    number = Slots()
    sent = []

    def start(src, dst, key, dev):
        i = number(*key)
        copy = pltpu.make_async_remote_copy(
            src_ref=src, dst_ref=dst, send_sem=send.at[i], recv_sem=recv.at[i],
            device_id=dev, device_id_type=MESH,
        )
        copy.start()
        sent.append(copy)

    def wait(dst, key):
        i = number(*key)
        pltpu.make_async_remote_copy(
            src_ref=dst, dst_ref=dst, send_sem=send.at[i], recv_sem=recv.at[i],
            device_id=core_dev, device_id_type=MESH,
        ).wait_recv()

    def x_dev(r):
        return {"dp": (d + r) % 4}

    barrier = pltpu.get_barrier_semaphore()
    near = [core_dev, z_dev] + [y_dev(r) for r in (1, 3, 2)]
    near += [{"dp": (d + r) % 4} for r in (1, 3, 2)] + [{"mp": (m + r) % 4} for r in (1, 2, 3)]
    for dev in near:
        pl.semaphore_signal(barrier, inc=1, device_id=dev, device_id_type=MESH)

    g_own = c * 4 + y
    t_load = pltpu.make_async_copy(tok, t_own.at[d], local.at[8])
    t_load.start()
    w_loads = {}

    def load_weight(cc):
        for rel in (2, 1, 3, 0):
            g = (c if cc == 0 else 1 - c) * 4 + (y + rel) % 4
            copy = pltpu.make_async_copy(
                wgt.at[:, pl.ds(pl.multiple_of(g * COLS, COLS), COLS)], w_own.at[g],
                local.at[rel * 2 + cc],
            )
            copy.start()
            w_loads[rel, cc] = copy

    load_weight(0)
    pl.semaphore_wait(barrier, len(near))

    for r in (1, 3, 2):
        start(tok, t_own.at[d], ("tok", r), x_dev(r))
    start(tok, t_peer.at[d], ("tpeer", 0), core_dev)
    for rel in (2, 1, 3, 0):
        yy = (y + rel) % 4
        g = (1 - c) * 4 + yy
        start(
            wgt.at[:, pl.ds(pl.multiple_of(g * COLS, COLS), COLS)], w_peer.at[yy],
            ("w", rel), core_dev,
        )
    c_load = pltpu.make_async_copy(
        cot.at[:, :, pl.ds(pl.multiple_of(g_own * COLS, COLS), COLS)], c_raw, local.at[9]
    )
    c_load.start()
    load_weight(1)
    r_load = pltpu.make_async_copy(row_mom, r_mom, local.at[10])
    r_load.start()
    m_load = pltpu.make_async_copy(col_mom, c_mom, local.at[11])
    m_load.start()
    for r in (1, 2, 3):
        pl.semaphore_signal(heard, inc=1, device_id={"mp": (m + r) % 4}, device_id_type=MESH)

    have_w = set()

    def product(k, rel):
        dk, yy = (d + k) % 4, (y + rel) % 4
        if rel not in have_w:
            have_w.add(rel)
            w_loads[rel, 0].wait()
            wait(w_peer.at[yy], ("w", rel))
        return jnp.dot(
            t_own[dk], w_own[c * 4 + yy], preferred_element_type=F32
        ) + jnp.dot(t_peer[dk], w_peer[yy], preferred_element_type=F32)

    def stage_tokens(k):
        dk = (d + k) % 4
        if k == 0:
            t_load.wait()
        else:
            wait(t_own.at[dk], ("tok", 4 - k))
            start(t_own.at[dk], t_peer.at[dk], ("tpeer", k), core_dev)

    def stage_products(k):
        dk = (d + k) % 4
        wait(t_peer.at[dk], ("tpeer", k))
        for rel in (2, 1, 3):
            so[k, rel - 1] = product(k, rel).astype(BF16)
            start(so.at[k, rel - 1], rr.at[k, rel - 1], ("rs", k, rel), y_dev(rel))
        ho[k] = product(k, 0)

    def stage_sum(k):
        total = ho[k]
        for rel in (1, 3, 2):
            wait(rr.at[k, rel - 1], ("rs", k, rel))
            total = total + rr[k, rel - 1].astype(F32)
        ho[k] = total
        zs[k] = total.astype(BF16)
        start(zs.at[k], zr.at[k], ("z", k), z_dev)

    def chunk_of(k):
        dk = (d + k) % 4
        return pl.ds(pl.multiple_of(dk * CHUNK, CHUNK), CHUNK)

    def stage_slope(k):
        dk = (d + k) % 4
        if k == 0:
            upstream = c_out[d]
        else:
            wait(ct.at[dk], ("ct", 4 - k))
            upstream = ct[dk]
        wait(zr.at[k], ("z", k))
        hidden = ho[k] + zr[k].astype(F32)
        sl[g_own, chunk_of(k)] = (upstream.astype(F32) * gelu_slope(hidden)).astype(BF16)
        block = sl.at[g_own, chunk_of(k)]
        start(block, block, ("core", 0, k), core_dev)
        for rel in (2, 1, 3):
            start(block, block, ("ag", rel, k), y_dev(rel))

    def stage_arrive(k):
        for rel in (1, 3, 2):
            block = sl.at[c * 4 + (y + 4 - rel) % 4, chunk_of(k)]
            wait(block, ("ag", rel, k))
            start(block, block, ("core", 4 - rel, k), core_dev)

    def group_at(rel, cc):
        return (c if cc == 0 else 1 - c) * 4 + (y + rel) % 4

    def group(rel, cc, sums):
        g = group_at(rel, cc)
        value = jnp.dot(t_tr[...], sl[g], preferred_element_type=F32)
        grad[g] = value
        squares = value * value + tiny_term
        sums[...] = jnp.sum(squares, axis=0, keepdims=True)
        lanes = squares[:, :128] + squares[:, 128:]
        if (rel, cc) == (0, 0):
            row_acc[...] = lanes
        else:
            row_acc[...] += lanes

    def stage_core(k, rels):
        for rel in rels:
            wait(sl.at[group_at(rel, 1), chunk_of(k)], ("core", rel, k))

    def input_terms(k):
        if k == 0:
            for rel in range(4):
                w_loads[rel, 1].wait()
        part = None
        for g in range(GROUPS):
            more = lax.dot_general(
                sl[g, chunk_of(k)], w_own[g], (((1,), (1,)), ((), ())), preferred_element_type=F32
            )
            part = more if part is None else part + more
        if k == 0:
            i_sum[...] = part
        else:
            i_out[k] = part.astype(BF16)
            start(i_out.at[k], i_in.at[k], ("ix", k), x_dev(k))

    late = []

    def settle(copies):
        for copy in copies:
            copy.wait_send()
        copies.clear()

    def peer_copy(buf, slot, base, j, dev):
        return pltpu.make_async_remote_copy(
            src_ref=buf.at[slot], dst_ref=buf.at[slot], send_sem=peer_send.at[base + j],
            recv_sem=peer_recv.at[base + j], device_id=dev, device_id_type=MESH,
        )

    def fsdp_dev(j):
        return {"fsdp": (f + j) % 16}

    def plane_dev(j):
        return {"dp": (d + j // 4) % 4, "mp": (m + j % 4) % 4}

    def to_fsdp(buf, slot, base):
        for j in FAR_FSDP:
            copy = peer_copy(buf, slot, base, j, fsdp_dev(j))
            copy.start()
            late.append(copy)

    def from_fsdp(buf, base):
        for j in FAR_FSDP[::-1]:
            peer_copy(buf, (f + 16 - j) % 16, base, j, fsdp_dev(j)).wait_recv()

    def to_plane(buf, slot, base):
        for j in FAR_PLANE:
            copy = peer_copy(buf, slot, base, j, plane_dev(j))
            copy.start()
            late.append(copy)

    z8 = (zh * 4 + m) * 2 + c

    def cross_dev(j):
        return {"dp": (d + j // 4) % 4, "fsdp": fid(zh, (y + j % 4) % 4, c)}

    def to_cross(buf, slot, base):
        for j in FAR_CROSS:
            copy = peer_copy(buf, slot, base, j, cross_dev(j))
            copy.start()
            late.append(copy)

    def from_cross(buf, base):
        for j in FAR_CROSS[::-1]:
            came = ((d + 4 - j // 4) % 4) * 4 + (y + 4 - j % 4) % 4
            peer_copy(buf, came, base, j, cross_dev(j)).wait_recv()

    def pole_dev(j):
        k = (z8 + j) % 16
        return {"fsdp": fid(k // 8, y, k % 2), "mp": (k // 2) % 4}

    def to_pole(buf, slot, base):
        for j in FAR_FSDP:
            copy = peer_copy(buf, slot, base, j, pole_dev(j))
            copy.start()
            late.append(copy)

    def from_pole(buf, base):
        for j in FAR_FSDP[::-1]:
            peer_copy(buf, (z8 + 16 - j) % 16, base, j, pole_dev(j)).wait_recv()

    def from_plane(buf, base):
        for j in FAR_PLANE[::-1]:
            came = ((d + 4 - j // 4) % 4) * 4 + (m + 4 - j % 4) % 4
            peer_copy(buf, came, base, j, plane_dev(j)).wait_recv()

    def transpose(k):
        dk = (d + k) % 4
        t_tr[:, pl.ds(pl.multiple_of(dk * CHUNK, CHUNK), CHUNK)] = t_own[dk].T

    stage_tokens(0)
    stage_products(0)
    c_load.wait()
    for b in range(4):
        c_out[b] = c_raw[:, b, :]
    stage_tokens(1)
    stage_tokens(3)
    stage_products(1)
    stage_products(3)
    stage_sum(0)
    stage_tokens(2)
    for r in (1, 3, 2):
        start(c_out.at[(d + r) % 4], ct.at[d], ("ct", r), x_dev(r))
    stage_products(2)
    stage_sum(1)
    for k in ORDER:
        transpose(k)
    stage_slope(0)
    stage_sum(3)
    stage_sum(2)
    stage_slope(1)
    stage_arrive(0)
    stage_slope(3)
    stage_slope(2)
    stage_arrive(1)
    stage_core(0, (0, 1, 3, 2))
    input_terms(0)
    group(0, 0, col_a.at[f, 0])
    stage_arrive(3)
    stage_core(1, (0,))
    stage_core(3, (0,))
    stage_core(2, (0,))
    group(0, 1, col_a.at[f, 1])
    stage_arrive(2)
    for i in range(2, 5):
        group(*FIRST[i], col_a.at[f, i])
    to_fsdp(col_a, f, 16)
    for k in (1, 3, 2):
        stage_core(k, (1, 3, 2))
    for i in range(3):
        group(*LAST[i], col_b.at[f, i])
    to_fsdp(col_b, f, 64)

    sent_before = list(sent)
    sent.clear()
    me = d * 4 + m
    row_buf[me] = jnp.sum(row_acc[...].T, axis=0, keepdims=True)

    pl.semaphore_wait(heard, 3)
    to_plane(row_buf, me, 0)
    for k in (2, 1, 3):
        input_terms(k)
    settle(sent_before)
    from_plane(row_buf, 0)
    total = row_buf[0]
    for j in range(1, 16):
        total = total + row_buf[j]
    r_load.wait()
    row_new = DECAY * r_mom[...] + (1.0 - DECAY) * total / HID
    row_out[...] = row_new
    rcol = jnp.broadcast_to(lax.rsqrt(row_new), (128, ROWS)).T
    row_acc[...] = rcol
    from_fsdp(col_a, 16)
    m_load.wait()

    def col_finish(own_core, yy):
        g = own_core * 4 + yy
        total = jnp.zeros((1, COLS), F32)
        for s in range(16):
            place = ((yy - s // 2) % 4, own_core ^ (s % 2))
            if place in FIRST:
                total = total + col_a[s, FIRST.index(place)]
            else:
                total = total + col_b[s, LAST.index(place)]
        col_out[g] = DECAY * c_mom[g] + (1.0 - DECAY) * total / D

    from_fsdp(col_b, 64)
    for own_core in (0, 1):
        for yy in range(4):
            col_finish(own_core, yy)

    def weigh(b, carry):
        rows = pl.ds(pl.multiple_of(b * 64, 64), 64)
        acc = jnp.zeros((64, 128), F32)
        for g in range(GROUPS):
            inverse = 1.0 / col_out[g]
            piece = grad[g, rows]
            piece = piece * piece * inverse
            acc = acc + piece[:, :128] + piece[:, 128:]
        right = row_acc[rows]
        return carry + jnp.sum(acc * (right * right), axis=0, keepdims=True)

    u_lanes = lax.fori_loop(0, 8, weigh, jnp.zeros((1, 128), F32))
    a_lanes = (row_new[:, :128] + row_new[:, 128:256]) + (row_new[:, 256:384] + row_new[:, 384:])
    here = d * 4 + y
    one_buf[z8, :, :128] = u_lanes
    one_buf[z8, :, 128:] = a_lanes
    sums_before = list(late)
    late.clear()
    to_pole(one_buf, z8, 32)

    acc = i_sum[...]
    for r in (1, 3, 2):
        wait(i_in.at[r], ("ix", r))
        acc = acc + i_in[r].astype(F32)
    i_sum[...] = acc
    for r in (1, 3, 2):
        mr = (m + r) % 4
        j_out[r] = i_sum[:, pl.ds(pl.multiple_of(mr * 128, 128), 128)].astype(BF16)
        start(j_out.at[r], j_in.at[r], ("jz", r), {"mp": mr})

    def spread_rows(b, carry):
        rows = pl.ds(pl.multiple_of(b * 64, 64), 64)
        left = row_acc[rows]
        for g in range(GROUPS):
            right = lax.rsqrt(col_out[g])
            for h in (0, 1):
                lanes = slice(h * 128, h * 128 + 128)
                shape[pl.ds(b * 1024 + 2 * g + h, 64, stride=16), :] = (
                    grad[g, rows, lanes] * left * right[:, lanes]
                )
        block = pl.ds(pl.multiple_of(b * 1024, 1024), 1024)
        pltpu.make_async_copy(shape.at[block], shape_out.at[block], peer_send.at[80 + b]).start()
        return carry

    lax.fori_loop(0, 8, spread_rows, 0)
    settle(sums_before)
    from_pole(one_buf, 32)
    total = one_buf[0]
    for j in range(1, 16):
        total = total + one_buf[j]
    two_buf[here] = total
    pole_before = list(late)
    late.clear()
    to_cross(two_buf, here, 48)
    settle(pole_before)
    settle(sent)

    def written(b, carry):
        block = pl.ds(pl.multiple_of(b * 1024, 1024), 1024)
        pltpu.make_async_copy(shape.at[block], shape_out.at[block], peer_send.at[80 + b]).wait()
        return carry

    lax.fori_loop(0, 8, written, 0)
    from_cross(two_buf, 48)
    total = two_buf[0]
    for j in range(1, 16):
        total = total + two_buf[j]
    scal_out[...] = total

    acc = i_sum[:, pl.ds(pl.multiple_of(m * 128, 128), 128)]
    for r in (1, 3, 2):
        wait(j_in.at[r], ("jz", r))
        acc = acc + j_in[r].astype(F32)
    inp_out[...] = acc.astype(BF16)

    for copy in sent + late:
        copy.wait_send()
    assert len(number.numbers) <= N_SEMS, len(number.numbers)


def last_kernel(shape, row_new, col_new, scal, inp, upd_out, row_out, col_out, inp_out, rms_out):
    total = jnp.sum(scal[:, :128], axis=1, keepdims=True)
    mean = jnp.sum(scal[:, 128:], axis=1, keepdims=True) / (16.0 * D)
    rms = jnp.sqrt(mean * total / (D * HID))
    factor = jnp.sqrt(mean) / jnp.maximum(1.0, rms / clip_level)
    upd_out[...] = shape[...] * factor

    @pl.when(pl.program_id(0) == 0)
    def _():
        row_out[...] = row_new[...]
        col_out[...] = col_new[...]
        inp_out[...] = inp[...]
        rms_out[...] = rms


def per_device(tokens_in, weight, cotangent, row_moment, col_moment):
    vmem = pl.BlockSpec(memory_space=pltpu.VMEM)
    hbm = pl.BlockSpec(memory_space=pltpu.HBM)
    sds = jax.ShapeDtypeStruct
    shape, inp, row_new, col_new, scal = pl.pallas_call(
        main_kernel,
        name="main",
        out_shape=(
            sds((ROWS * 16, 128), F32),
            sds((CHUNK, 128), BF16),
            sds((1, ROWS), F32),
            sds((GROUPS, 1, COLS), F32),
            sds((1, 256), F32),
        ),
        in_specs=[hbm] * 5,
        out_specs=(hbm, vmem, vmem, vmem, vmem),
        scratch_shapes=[
            pltpu.VMEM((4, CHUNK, ROWS), BF16),
            pltpu.VMEM((4, CHUNK, ROWS), BF16),
            pltpu.VMEM((ROWS, 4 * CHUNK), BF16),
            pltpu.VMEM((GROUPS, ROWS, COLS), BF16),
            pltpu.VMEM((4, ROWS, COLS), BF16),
            pltpu.VMEM((CHUNK, 4, COLS), BF16),
            pltpu.VMEM((4, CHUNK, COLS), BF16),
            pltpu.VMEM((4, CHUNK, COLS), BF16),
            pltpu.VMEM((4, 3, CHUNK, COLS), BF16),
            pltpu.VMEM((4, 3, CHUNK, COLS), BF16),
            pltpu.VMEM((4, CHUNK, COLS), F32),
            pltpu.VMEM((4, CHUNK, COLS), BF16),
            pltpu.VMEM((4, CHUNK, COLS), BF16),
            pltpu.VMEM((GROUPS, 4 * CHUNK, COLS), BF16),
            pltpu.VMEM((GROUPS, ROWS, COLS), F32),
            pltpu.VMEM((ROWS * 16, 128), F32),
            pltpu.VMEM((4, CHUNK, ROWS), BF16),
            pltpu.VMEM((4, CHUNK, ROWS), BF16),
            pltpu.VMEM((CHUNK, ROWS), F32),
            pltpu.VMEM((4, CHUNK, 128), BF16),
            pltpu.VMEM((4, CHUNK, 128), BF16),
            pltpu.VMEM((1, ROWS), F32),
            pltpu.VMEM((GROUPS, 1, COLS), F32),
            pltpu.VMEM((ROWS, 128), F32),
            pltpu.VMEM((16, 1, ROWS), F32),
            pltpu.VMEM((16, 5, 1, COLS), F32),
            pltpu.VMEM((16, 3, 1, COLS), F32),
            pltpu.VMEM((16, 1, 256), F32),
            pltpu.VMEM((16, 1, 256), F32),
            pltpu.SemaphoreType.DMA((N_SEMS,)),
            pltpu.SemaphoreType.DMA((N_SEMS,)),
            pltpu.SemaphoreType.DMA((12,)),
            pltpu.SemaphoreType.DMA((88,)),
            pltpu.SemaphoreType.DMA((88,)),
            pltpu.SemaphoreType.REGULAR,
        ],
        compiler_params=pltpu.CompilerParams(
            collective_id=0, has_side_effects=True, vmem_limit_bytes=60 * 1024 * 1024
        ),
        cost_estimate=pl.CostEstimate(flops=3 * 2**30, bytes_accessed=8 * 2**20, transcendentals=2**16),
    )(
        tokens_in,
        weight.reshape(ROWS, GROUPS * COLS),
        cotangent,
        row_moment.reshape(1, ROWS),
        col_moment.reshape(GROUPS, 1, COLS),
    )
    steps = 2
    rows = ROWS // steps
    whole = lambda *shape: pl.BlockSpec(shape, lambda i: (0,) * len(shape))
    update, row_new, col_new, input_grad, rms = pl.pallas_call(
        last_kernel,
        name="last",
        grid=(steps,),
        out_shape=(
            sds((ROWS * 16, 128), F32),
            sds((1, ROWS), F32),
            sds((GROUPS, 1, COLS), F32),
            sds((CHUNK, 128), BF16),
            sds((1, 1), F32),
        ),
        in_specs=[
            pl.BlockSpec((rows * 16, 128), lambda i: (i, 0)),
            whole(1, ROWS),
            whole(GROUPS, 1, COLS),
            whole(1, 256),
            whole(CHUNK, 128),
        ],
        out_specs=(
            pl.BlockSpec((rows * 16, 128), lambda i: (i, 0)),
            whole(1, ROWS),
            whole(GROUPS, 1, COLS),
            whole(CHUNK, 128),
            whole(1, 1),
        ),
        compiler_params=pltpu.CompilerParams(vmem_limit_bytes=60 * 1024 * 1024),
    )(shape, row_new, col_new, scal, inp)
    return (
        input_grad,
        row_new.reshape(ROWS),
        col_new.reshape(1, GROUPS * COLS),
        update.reshape(ROWS, 1, GROUPS * COLS),
        rms.reshape(()),
    )


def solution(mesh):
    in_specs = (
        P("dp", "fsdp"),
        P("fsdp", "dp", "mp"),
        P("dp", None, "mp"),
        P("fsdp"),
        P("dp", "mp"),
    )
    out_specs = (P("dp", ("fsdp", "mp")), P("fsdp"), P("dp", "mp"), P("fsdp", "dp", "mp"), P())
    return jax.shard_map(
        per_device, mesh=mesh, in_specs=in_specs, out_specs=out_specs, check_vma=False
    )
```
